256 devices in a mesh: wide: 64 (over x_lo, z, y), narrow: 4 (over x_hi, core).
Axes of the slice: x: 4 (x_hi: 2, x_lo: 2; x = x_hi * 2 + x_lo), y: 4, z: 8, core: 2. Of those that a mesh axis runs over, the one named last changes fastest.
Arguments:
- samples: bfloat16 [1024, 396288], P(('narrow', 'wide')), may hold values from -6 to 6
- pfb_taps: float32 [4, 1024], replicated, may hold values from -3 to 3
Outputs:
- self_vis: float32 [2, 512, 1024, 256], P(None, 'wide', 'narrow')
- prior_vis: float32 [2, 512, 1024, 256], P(None, 'wide', 'narrow')
- far_vis: float32 [2, 512, 1024, 128], P(None, 'wide', 'narrow')
The draws below stay inside these ranges and needn't reach their ends.
All inputs are finite; a program needn't handle non-finite values.
Results may differ from the reference program's by a relative error of at most 0.0065.
Values may be sent and summed in bfloat16 or wider, within the bound.
No kernel may reach another device: no remote copies, remote signals or barrier semaphores. Data moves between devices by JAX's collectives and lax.ppermute only.
A program may use at most 128 MiB of HBM per device.

```python
import math
import jax
import jax.numpy as jnp
from jax import lax

INPUTS = 1024
CHAN = 512
TAPS = 4
SPECTRA = 384
BLOCK = 256
N_NARROW = 4


def block_levels(own_key, extent, pieces, least, largest):
    gain = 1.0
    for axis_at, shards_of in pieces:
        draws = jax.random.uniform(jax.random.fold_in(jax.random.fold_in(own_key, 6), axis_at), (shards_of,), jnp.float32, least / len(pieces), largest / len(pieces))
        gain = gain * jnp.repeat(jnp.exp(draws), extent[axis_at] // shards_of).reshape((-1,) + (1,) * (len(extent) - 1 - axis_at))
    return gain


def normal_values(own_key, extent, width, reach, cuts=(), kind=jnp.bfloat16):
    values = jax.random.normal(own_key, extent, jnp.float32) * width
    if len(cuts) > 0:
        values = block_levels(own_key, extent, cuts, -0.22, 0.18) * values
    return jnp.clip(values, min=-reach, max=reach).astype(kind)


def setup_inputs(seed: int = 0) -> dict:
    key_list = jax.random.split(jax.random.key(seed), 3)
    samples = normal_values(key_list[0], (INPUTS, (SPECTRA + TAPS - 1) * 2 * CHAN), 1.0, 6.0, ((0, 256),))
    pfb_taps = normal_values(key_list[1], (TAPS, 2 * CHAN), 0.5, 3.0, (), jnp.float32)
    return {"samples": samples, "pfb_taps": pfb_taps}


def dft_table(channels):
    positions = jnp.arange(2 * channels, dtype=jnp.int32)
    bins = jnp.arange(channels, dtype=jnp.int32)
    phases = (bins[:, None] * positions[None, :]) % (2 * channels)
    angles = phases.astype(jnp.float32) * (math.pi / channels)
    norming = (2.0 * channels) ** -0.5
    return jnp.stack([jnp.cos(angles) * norming, -jnp.sin(angles) * norming]).astype(jnp.bfloat16)


def polyphase(shaped, pfb_taps, spectra):
    total = jnp.zeros((shaped.shape[0], spectra, shaped.shape[2]), jnp.float32)
    for tap_index in range(pfb_taps.shape[0]):
        total = total + shaped[:, tap_index:tap_index + spectra, :].astype(jnp.float32) * pfb_taps[tap_index]
    return total.astype(jnp.bfloat16)


def cross_tile(row_block, col_block):
    rows_f = row_block.astype(jnp.float32)
    cols_f = col_block.astype(jnp.float32)
    real_part = jnp.einsum("cik,cjk->cij", rows_f, cols_f)
    turned = jnp.concatenate([rows_f[..., SPECTRA:], -rows_f[..., :SPECTRA]], axis=-1)
    imag_part = jnp.einsum("cik,cjk->cij", turned, cols_f)
    return jnp.stack([real_part, imag_part]) / SPECTRA


def reference(samples, pfb_taps):
    frames = SPECTRA + TAPS - 1
    table = dft_table(CHAN).astype(jnp.float32)
    groups = samples.reshape(INPUTS // 16, 16, frames, 2 * CHAN)

    def transform(group):
        filtered = polyphase(group, pfb_taps, SPECTRA)
        return jnp.einsum("pcn,isn->cips", table, filtered.astype(jnp.float32)).astype(jnp.bfloat16)

    spectra = lax.map(transform, groups)
    spectra = jnp.transpose(spectra, (1, 0, 2, 3, 4)).reshape(CHAN, INPUTS, 2 * SPECTRA)
    blocks = spectra.reshape(CHAN, N_NARROW, BLOCK, 2 * SPECTRA)
    halfway = BLOCK // 2
    self_parts = []
    prior_parts = []
    far_parts = []
    for position in range(N_NARROW):
        self_parts.append(cross_tile(blocks[:, position], blocks[:, position]))
        prior_parts.append(cross_tile(blocks[:, position], blocks[:, (position + 3) % N_NARROW]))
        far_cols = blocks[:, (position + 2) % N_NARROW, (position // 2) * halfway:(position // 2 + 1) * halfway]
        far_parts.append(cross_tile(blocks[:, position], far_cols))
    return (jnp.concatenate(self_parts, axis=2), jnp.concatenate(prior_parts, axis=2), jnp.concatenate(far_parts, axis=2))
```

```python
import functools
import math

import jax
import jax.numpy as jnp
import numpy as np
from jax import lax
from jax.experimental import pallas as pl
from jax.experimental.pallas import tpu as pltpu
from jax.sharding import PartitionSpec as P

CHAN = 512
TAPS = 4
SPECTRA = 384
BLOCK = 256
FRAME = 2 * CHAN
SB = 128
NT = (((1,), (1,)), ((), ()))


def dft_table():
    positions = np.arange(FRAME, dtype=np.int32)
    bins = np.arange(CHAN, dtype=np.int32)
    phases = bins[:, None] * positions[None, :] % FRAME
    angles = phases.astype(np.float32) * np.float32(math.pi / CHAN)
    norming = np.float32(FRAME ** (-0.5))
    table = np.concatenate([np.cos(angles) * norming, -np.sin(angles) * norming])
    return table.astype(jnp.bfloat16)


def row_order():
    order = np.arange(256).reshape(32, 8).T.reshape(-1)
    return np.eye(256, dtype=np.float32)[order].astype(jnp.bfloat16)


def spectra_kernel(x_ref, halo_ref, taps_ref, table_ref, out_ref, frames, filtered):
    for f in range(SB):
        for n in range(0, FRAME, 128):
            frames[n // 128, 4 * f : 4 * f + 4, :] = x_ref[:, f * FRAME + n : f * FRAME + n + 128].astype(jnp.float32)
    for f in range(TAPS - 1):
        for n in range(0, FRAME, 128):
            frames[n // 128, 4 * (SB + f) : 4 * (SB + f) + 4, :] = halo_ref[
                :, f * FRAME + n : f * FRAME + n + 128
            ].astype(jnp.float32)
    for n in range(0, FRAME, 128):
        taps = [taps_ref[t : t + 1, n : n + 128] for t in range(TAPS)]
        for i in range(4):
            for s in range(0, SB, 16):
                total = frames[n // 128, pl.ds(i + 4 * s, 16, stride=4), :] * taps[0]
                for t in range(1, TAPS):
                    total = total + frames[n // 128, pl.ds(i + 4 * (s + t), 16, stride=4), :] * taps[t]
                filtered[i * SB + s : i * SB + s + 16, n : n + 128] = total.astype(jnp.bfloat16)
    for pair in range(2):
        product = lax.dot_general(
            table_ref[...], filtered[pair * 2 * SB : (pair + 1) * 2 * SB, :], NT,
            preferred_element_type=jnp.float32,
        )
        for p in range(2):
            part = product[p * CHAN : (p + 1) * CHAN]
            rows = jnp.concatenate(
                [part[:, :SB].reshape(CHAN // 8, 8, SB), part[:, SB:].reshape(CHAN // 8, 8, SB)], axis=1
            )
            out_ref[:, pair * 16 : pair * 16 + 16, p * SB : (p + 1) * SB] = rows.astype(jnp.bfloat16)


def filter_section(samples, pfb_taps, table, first, count):
    return pl.pallas_call(
        spectra_kernel,
        grid=(count,),
        in_specs=[
            pl.BlockSpec((4, SB * FRAME), lambda j: (0, first + j)),
            pl.BlockSpec((4, 4 * FRAME), lambda j: (0, (first + j + 1) * (SB // 4))),
            pl.BlockSpec((TAPS, FRAME), lambda j: (0, 0)),
            pl.BlockSpec((2 * CHAN, FRAME), lambda j: (0, 0)),
        ],
        out_specs=pl.BlockSpec((64, 32, 2 * SB), lambda j: (0, 0, j)),
        out_shape=jax.ShapeDtypeStruct((64, 32, count * 2 * SB), jnp.bfloat16),
        scratch_shapes=[
            pltpu.VMEM((FRAME // 128, 4 * (SB + 4), 128), jnp.float32),
            pltpu.VMEM((4 * SB, FRAME), jnp.bfloat16),
        ],
        compiler_params=pltpu.CompilerParams(vmem_limit_bytes=40 * 1024 * 1024),
        name="filter_section",
    )(samples, samples, pfb_taps, table)


def reorder(order, source, out_ref, groups, lane):
    width = source.shape[-1]
    for g in range(groups):
        rows = source[g * 8 : (g + 1) * 8].reshape(256, width)
        turned = jnp.dot(order, rows, preferred_element_type=jnp.float32).astype(jnp.bfloat16)
        for c in range(8):
            out_ref[c, g * 32 : (g + 1) * 32, lane : lane + width] = turned[c * 32 : (c + 1) * 32]


def stacked(rows):
    pieces = []
    for s in range(0, rows.shape[1], 2 * SB):
        pieces += [rows[:, s + SB : s + 2 * SB], -rows[:, s : s + SB]]
    return jnp.concatenate([rows, jnp.concatenate(pieces, axis=1)], axis=0)


def self_kernel(order_ref, own0_ref, own1_ref, own_ref, self_ref, held):
    step = pl.program_id(0)

    @pl.when(step == 0)
    def _():
        reorder(order_ref[...], own0_ref, held, 8, 0)
        reorder(order_ref[...], own1_ref, held, 8, 512)

    rows = held[step]
    own_ref[0] = rows
    product = lax.dot_general(stacked(rows), rows, NT, preferred_element_type=jnp.float32) * (1.0 / SPECTRA)
    self_ref[0, 0] = product[:BLOCK]
    self_ref[1, 0] = product[BLOCK:]


def self_tiles(order, own0, own1):
    whole = lambda a: pl.BlockSpec(a.shape, lambda c: (0,) * a.ndim)
    return pl.pallas_call(
        self_kernel,
        grid=(8,),
        in_specs=[whole(order), whole(own0), whole(own1)],
        out_specs=[
            pl.BlockSpec((1, BLOCK, 768), lambda c: (c, 0, 0)),
            pl.BlockSpec((2, 1, BLOCK, BLOCK), lambda c: (0, c, 0, 0)),
        ],
        out_shape=[
            jax.ShapeDtypeStruct((8, BLOCK, 768), jnp.bfloat16),
            jax.ShapeDtypeStruct((2, 8, BLOCK, BLOCK), jnp.float32),
        ],
        scratch_shapes=[pltpu.VMEM((8, BLOCK, 768), jnp.bfloat16)],
        compiler_params=pltpu.CompilerParams(vmem_limit_bytes=40 * 1024 * 1024),
        name="self_tiles",
    )(order, own0, own1)


def cross_kernel(order_ref, own_ref, prior0_ref, prior1_ref, fare0_ref, fare1_ref, faro0_ref, faro1_ref,
                 prior_ref, far_ref, held):
    step = pl.program_id(0)

    @pl.when(step == 0)
    def _():
        order = order_ref[...]
        reorder(order, prior0_ref, held, 8, 0)
        reorder(order, prior1_ref, held, 8, 512)
        far_held = held.at[:, BLOCK : BLOCK + BLOCK // 2]
        reorder(order, fare0_ref[...] + faro0_ref[...], far_held, 4, 0)
        reorder(order, fare1_ref[...] + faro1_ref[...], far_held, 4, 512)

    product = lax.dot_general(stacked(own_ref[0]), held[step], NT, preferred_element_type=jnp.float32) * (1.0 / SPECTRA)
    prior_ref[0, 0] = product[:BLOCK, :BLOCK]
    prior_ref[1, 0] = product[BLOCK:, :BLOCK]
    far_ref[0, 0] = product[:BLOCK, BLOCK:]
    far_ref[1, 0] = product[BLOCK:, BLOCK:]


def cross_tiles(order, own, *received):
    whole = lambda a: pl.BlockSpec(a.shape, lambda c: (0,) * a.ndim)
    return pl.pallas_call(
        cross_kernel,
        grid=(8,),
        in_specs=[whole(order), pl.BlockSpec((1, BLOCK, 768), lambda c: (c, 0, 0))] + [whole(a) for a in received],
        out_specs=[
            pl.BlockSpec((2, 1, BLOCK, BLOCK), lambda c: (0, c, 0, 0)),
            pl.BlockSpec((2, 1, BLOCK, BLOCK // 2), lambda c: (0, c, 0, 0)),
        ],
        out_shape=[
            jax.ShapeDtypeStruct((2, 8, BLOCK, BLOCK), jnp.float32),
            jax.ShapeDtypeStruct((2, 8, BLOCK, BLOCK // 2), jnp.float32),
        ],
        scratch_shapes=[pltpu.VMEM((8, BLOCK + BLOCK // 2, 768), jnp.bfloat16)],
        compiler_params=pltpu.CompilerParams(vmem_limit_bytes=48 * 1024 * 1024),
        name="cross_tiles",
    )(order, own, *received)


PRIOR = [(0, 1), (1, 2), (2, 3), (3, 0)]
FAR_EVEN = [(0, 2), (2, 0)]
FAR_ODD = [(0, 1), (2, 3)]


def on_device(table, order, samples, pfb_taps):
    chip = lax.axis_index("narrow") // 2
    chunks = [filter_section(samples, pfb_taps, table, 0, 2), filter_section(samples, pfb_taps, table, 2, 1)]
    own, prior, far_even, far_odd = [], [], [], []
    for chunk in chunks:
        local = lax.all_to_all(chunk, "wide", split_axis=0, concat_axis=0, tiled=True)
        own.append(local)
        before = lax.ppermute(local, "narrow", PRIOR)
        prior.append(before)
        leaving = lax.dynamic_slice_in_dim(local, (1 - chip) * 32, 32, 0)
        far_even.append(lax.ppermute(leaving, "narrow", FAR_EVEN))
        passed = lax.dynamic_slice_in_dim(before, chip * 32, 32, 0)
        far_odd.append(lax.ppermute(passed, "narrow", FAR_ODD))
    mine, self_vis = self_tiles(order, *own)
    prior_vis, far_vis = cross_tiles(order, mine, *prior, *far_even, *far_odd)
    return (self_vis, prior_vis, far_vis)


def solution(mesh):
    return jax.shard_map(
        functools.partial(on_device, dft_table(), row_order()),
        mesh=mesh,
        in_specs=(P(("narrow", "wide"), None), P()),
        out_specs=(
            P(None, "wide", "narrow", None),
            P(None, "wide", "narrow", None),
            P(None, "wide", "narrow", None),
        ),
        check_vma=False,
    )
```

```python
import functools
import math

import jax
import jax.numpy as jnp
import numpy as np
from jax import lax
from jax.experimental import pallas as pl
from jax.experimental.pallas import tpu as pltpu
from jax.sharding import PartitionSpec as P

CHAN = 512
TAPS = 4
SPECTRA = 384
BLOCK = 256
FRAME = 2 * CHAN
SB = 128
NT = (((1,), (1,)), ((), ()))


def dft_table():
    positions = np.arange(FRAME, dtype=np.int32)
    bins = np.arange(CHAN, dtype=np.int32)
    phases = bins[:, None] * positions[None, :] % FRAME
    angles = phases.astype(np.float32) * np.float32(math.pi / CHAN)
    norming = np.float32(FRAME ** (-0.5))
    table = np.concatenate([np.cos(angles) * norming, -np.sin(angles) * norming])
    return table.astype(jnp.bfloat16)


def row_order():
    order = np.arange(256).reshape(32, 8).T.reshape(-1)
    return np.eye(256, dtype=np.float32)[order].astype(jnp.bfloat16)


def spectra_kernel(first, x_ref, table_ref, taps_ref, out_ref, x_held, table, frames, filtered, out_held, x_sem, table_sem, out_sem):
    count = x_held.shape[0]
    span = (SB + TAPS - 1) * FRAME
    arriving = [
        pltpu.make_async_copy(x_ref.at[:, pl.ds((first + j) * SB * FRAME, span)], x_held.at[j], x_sem.at[j])
        for j in range(count)
    ]
    table_arriving = pltpu.make_async_copy(table_ref, table, table_sem)
    arriving[0].start()
    table_arriving.start()
    for copy in arriving[1:]:
        copy.start()
    leaving = []
    for j in range(count):
        arriving[j].wait()
        for f in range(SB + TAPS - 1):
            for n in range(0, FRAME, 128):
                frames[n // 128, 4 * f : 4 * f + 4, :] = x_held[
                    j, :, f * FRAME + n : f * FRAME + n + 128
                ].astype(jnp.float32)
        for n in range(0, FRAME, 128):
            taps = [taps_ref[t : t + 1, n : n + 128] for t in range(TAPS)]
            for i in range(4):
                for s in range(0, SB, 16):
                    total = frames[n // 128, pl.ds(i + 4 * s, 16, stride=4), :] * taps[0]
                    for t in range(1, TAPS):
                        total = total + frames[n // 128, pl.ds(i + 4 * (s + t), 16, stride=4), :] * taps[t]
                    filtered[i * SB + s : i * SB + s + 16, n : n + 128] = total.astype(jnp.bfloat16)
        if j == 0:
            table_arriving.wait()
        for pair in range(2):
            product = lax.dot_general(
                table[...], filtered[pair * 2 * SB : (pair + 1) * 2 * SB, :], NT,
                preferred_element_type=jnp.float32,
            )
            for p in range(2):
                part = product[p * CHAN : (p + 1) * CHAN]
                rows = jnp.concatenate(
                    [part[:, :SB].reshape(CHAN // 8, 8, SB), part[:, SB:].reshape(CHAN // 8, 8, SB)], axis=1
                )
                out_held[j, :, pair * 16 : pair * 16 + 16, p * SB : (p + 1) * SB] = rows.astype(jnp.bfloat16)
        copy = pltpu.make_async_copy(
            out_held.at[j], out_ref.at[:, :, pl.ds(j * 2 * SB, 2 * SB)], out_sem.at[j]
        )
        copy.start()
        leaving.append(copy)
    for copy in leaving:
        copy.wait()


def filter_section(samples, pfb_taps, table, first, count):
    in_hbm = pl.BlockSpec(memory_space=pltpu.HBM)
    return pl.pallas_call(
        functools.partial(spectra_kernel, first),
        in_specs=[in_hbm, in_hbm, pl.BlockSpec(memory_space=pltpu.VMEM)],
        out_specs=in_hbm,
        out_shape=jax.ShapeDtypeStruct((64, 32, count * 2 * SB), jnp.bfloat16),
        scratch_shapes=[
            pltpu.VMEM((count, 4, (SB + TAPS - 1) * FRAME), jnp.bfloat16),
            pltpu.VMEM((2 * CHAN, FRAME), jnp.bfloat16),
            pltpu.VMEM((FRAME // 128, 4 * (SB + 4), 128), jnp.float32),
            pltpu.VMEM((4 * SB, FRAME), jnp.bfloat16),
            pltpu.VMEM((count, 64, 32, 2 * SB), jnp.bfloat16),
            pltpu.SemaphoreType.DMA((count,)),
            pltpu.SemaphoreType.DMA,
            pltpu.SemaphoreType.DMA((count,)),
        ],
        compiler_params=pltpu.CompilerParams(vmem_limit_bytes=40 * 1024 * 1024),
        name="filter_section",
    )(samples, table, pfb_taps)


def reorder(order, source, out_ref, groups, lane):
    width = source.shape[-1]
    for g in range(groups):
        rows = source[g * 8 : (g + 1) * 8].reshape(256, width)
        turned = jnp.dot(order, rows, preferred_element_type=jnp.float32).astype(jnp.bfloat16)
        for c in range(8):
            out_ref[c, g * 32 : (g + 1) * 32, lane : lane + width] = turned[c * 32 : (c + 1) * 32]


def stacked(rows):
    pieces = []
    for s in range(0, rows.shape[1], 2 * SB):
        pieces += [rows[:, s + SB : s + 2 * SB], -rows[:, s : s + SB]]
    return jnp.concatenate([rows, jnp.concatenate(pieces, axis=1)], axis=0)


def self_kernel(order_ref, own0_ref, own1_ref, own_ref, self_ref, held):
    step = pl.program_id(0)

    @pl.when(step == 0)
    def _():
        reorder(order_ref[...], own0_ref, held, 8, 0)
        reorder(order_ref[...], own1_ref, held, 8, 512)

    rows = held[step]
    own_ref[0] = rows
    product = lax.dot_general(stacked(rows), rows, NT, preferred_element_type=jnp.float32) * (1.0 / SPECTRA)
    self_ref[0, 0] = product[:BLOCK]
    self_ref[1, 0] = product[BLOCK:]


def self_tiles(order, own0, own1):
    whole = lambda a: pl.BlockSpec(a.shape, lambda c: (0,) * a.ndim)
    return pl.pallas_call(
        self_kernel,
        grid=(8,),
        in_specs=[whole(order), whole(own0), whole(own1)],
        out_specs=[
            pl.BlockSpec((1, BLOCK, 768), lambda c: (c, 0, 0)),
            pl.BlockSpec((2, 1, BLOCK, BLOCK), lambda c: (0, c, 0, 0)),
        ],
        out_shape=[
            jax.ShapeDtypeStruct((8, BLOCK, 768), jnp.bfloat16),
            jax.ShapeDtypeStruct((2, 8, BLOCK, BLOCK), jnp.float32),
        ],
        scratch_shapes=[pltpu.VMEM((8, BLOCK, 768), jnp.bfloat16)],
        compiler_params=pltpu.CompilerParams(vmem_limit_bytes=40 * 1024 * 1024),
        name="self_tiles",
    )(order, own0, own1)


def early_kernel(order_ref, prior_ref, fare_ref, faro_ref, out_ref):
    step = pl.program_id(0)

    @pl.when(step < 8)
    def _():
        reorder(order_ref[...], prior_ref, out_ref, 1, 0)

    @pl.when(step >= 8)
    def _():
        reorder(order_ref[...], fare_ref[...] + faro_ref[...], out_ref, 1, 0)


def early_columns(order, prior, far_even, far_odd):
    width = prior.shape[-1]
    far_spec = pl.BlockSpec((8, 32, width), lambda g: (jnp.maximum(g - 8, 0), 0, 0))
    return pl.pallas_call(
        early_kernel,
        grid=(12,),
        in_specs=[
            pl.BlockSpec(order.shape, lambda g: (0, 0)),
            pl.BlockSpec((8, 32, width), lambda g: (jnp.minimum(g, 7), 0, 0)),
            far_spec,
            far_spec,
        ],
        out_specs=pl.BlockSpec((8, 32, width), lambda g: (0, g, 0)),
        out_shape=jax.ShapeDtypeStruct((8, BLOCK + BLOCK // 2, width), jnp.bfloat16),
        compiler_params=pltpu.CompilerParams(vmem_limit_bytes=40 * 1024 * 1024),
        name="early_columns",
    )(order, prior, far_even, far_odd)


def cross_kernel(order_ref, own_ref, early_ref, late_prior_ref, late_fare_ref, late_faro_ref, prior_ref, far_ref, held):
    step = pl.program_id(0)
    width = early_ref.shape[-1]

    @pl.when(step == 0)
    def _():
        order = order_ref[...]
        reorder(order, late_prior_ref, held, 8, 0)
        reorder(order, late_fare_ref[...] + late_faro_ref[...], held.at[:, BLOCK : BLOCK + BLOCK // 2], 4, 0)

    rows = stacked(own_ref[0])
    product = lax.dot_general(rows[:, :width], early_ref[0], NT, preferred_element_type=jnp.float32)
    product += lax.dot_general(rows[:, width:], held[step], NT, preferred_element_type=jnp.float32)
    product *= 1.0 / SPECTRA
    prior_ref[0, 0] = product[:BLOCK, :BLOCK]
    prior_ref[1, 0] = product[BLOCK:, :BLOCK]
    far_ref[0, 0] = product[:BLOCK, BLOCK:]
    far_ref[1, 0] = product[BLOCK:, BLOCK:]


def cross_tiles(order, own, early, *late):
    whole = lambda a: pl.BlockSpec(a.shape, lambda c: (0,) * a.ndim)
    channel = lambda a: pl.BlockSpec((1,) + a.shape[1:], lambda c: (c, 0, 0))
    return pl.pallas_call(
        cross_kernel,
        grid=(8,),
        in_specs=[whole(order), channel(own), channel(early)] + [whole(a) for a in late],
        out_specs=[
            pl.BlockSpec((2, 1, BLOCK, BLOCK), lambda c: (0, c, 0, 0)),
            pl.BlockSpec((2, 1, BLOCK, BLOCK // 2), lambda c: (0, c, 0, 0)),
        ],
        out_shape=[
            jax.ShapeDtypeStruct((2, 8, BLOCK, BLOCK), jnp.float32),
            jax.ShapeDtypeStruct((2, 8, BLOCK, BLOCK // 2), jnp.float32),
        ],
        scratch_shapes=[pltpu.VMEM((8, BLOCK + BLOCK // 2, late[0].shape[-1]), jnp.bfloat16)],
        compiler_params=pltpu.CompilerParams(vmem_limit_bytes=48 * 1024 * 1024),
        name="cross_tiles",
    )(order, own, early, *late)


PRIOR = [(0, 1), (1, 2), (2, 3), (3, 0)]
FAR_EVEN = [(0, 2), (2, 0)]
FAR_ODD = [(0, 1), (2, 3)]


def on_device(table, order, samples, pfb_taps):
    chip = lax.axis_index("narrow") // 2
    early = filter_section(samples, pfb_taps, table, 0, 2)
    late = filter_section(samples, pfb_taps, table, 2, 1)

    def far_leaving(local):
        return lax.dynamic_slice_in_dim(local, (1 - chip) * 32, 32, 0)

    def far_passed(before):
        return lax.dynamic_slice_in_dim(before, chip * 32, 32, 0)

    own0 = lax.all_to_all(early, "wide", split_axis=0, concat_axis=0, tiled=True)
    late, own0 = lax.optimization_barrier((late, own0))
    own1 = lax.all_to_all(late, "wide", split_axis=0, concat_axis=0, tiled=True)
    prior0 = lax.ppermute(own0, "narrow", PRIOR)
    far_even0 = lax.ppermute(far_leaving(own0), "narrow", FAR_EVEN)
    far_odd0 = lax.ppermute(far_passed(prior0), "narrow", FAR_ODD)
    held0 = early_columns(order, prior0, far_even0, far_odd0)
    own1, held0 = lax.optimization_barrier((own1, held0))
    prior1 = lax.ppermute(own1, "narrow", PRIOR)
    far_even1 = lax.ppermute(far_leaving(own1), "narrow", FAR_EVEN)
    mine, self_vis = self_tiles(order, own0, own1)
    prior1, mine = lax.optimization_barrier((prior1, mine))
    far_odd1 = lax.ppermute(far_passed(prior1), "narrow", FAR_ODD)
    prior_vis, far_vis = cross_tiles(order, mine, held0, prior1, far_even1, far_odd1)
    return (self_vis, prior_vis, far_vis)


def solution(mesh):
    return jax.shard_map(
        functools.partial(on_device, dft_table(), row_order()),
        mesh=mesh,
        in_specs=(P(("narrow", "wide"), None), P()),
        out_specs=(
            P(None, "wide", "narrow", None),
            P(None, "wide", "narrow", None),
            P(None, "wide", "narrow", None),
        ),
        check_vma=False,
    )
```

```python
import functools
import math

import jax
import jax.numpy as jnp
import numpy as np
from jax import lax
from jax.experimental import pallas as pl
from jax.experimental.pallas import tpu as pltpu
from jax.sharding import PartitionSpec as P

CHAN = 512
TAPS = 4
SPECTRA = 384
BLOCK = 256
FRAME = 2 * CHAN
HALF = SPECTRA // 2
LANES = 2 * HALF
NT = (((1,), (1,)), ((), ()))


def dft_table():
    positions = np.arange(FRAME, dtype=np.int32)
    bins = np.arange(CHAN, dtype=np.int32)
    phases = bins[:, None] * positions[None, :] % FRAME
    angles = phases.astype(np.float32) * np.float32(math.pi / CHAN)
    norming = np.float32(FRAME ** (-0.5))
    table = np.concatenate([np.cos(angles) * norming, -np.sin(angles) * norming])
    return table.astype(jnp.bfloat16)


def row_order():
    order = np.arange(256).reshape(32, 8).T.reshape(-1)
    return np.eye(256, dtype=np.float32)[order].astype(jnp.bfloat16)


def spectra_kernel(first, x_ref, table_ref, taps_ref, out_ref, x_held, table, frames, filtered, out_held, x_sem, table_sem, out_sem):
    arriving = pltpu.make_async_copy(
        x_ref.at[:, pl.ds(first * FRAME, (HALF + TAPS - 1) * FRAME)], x_held, x_sem
    )
    table_arriving = pltpu.make_async_copy(table_ref, table, table_sem)
    arriving.start()
    table_arriving.start()
    arriving.wait()
    for f in range(HALF + TAPS - 1):
        for n in range(0, FRAME, 128):
            frames[n // 128, 4 * f : 4 * f + 4, :] = x_held[:, f * FRAME + n : f * FRAME + n + 128].astype(jnp.float32)
    for n in range(0, FRAME, 128):
        taps = [taps_ref[t : t + 1, n : n + 128] for t in range(TAPS)]
        for i in range(4):
            for s in range(0, HALF, 16):
                total = frames[n // 128, pl.ds(i + 4 * s, 16, stride=4), :] * taps[0]
                for t in range(1, TAPS):
                    total = total + frames[n // 128, pl.ds(i + 4 * (s + t), 16, stride=4), :] * taps[t]
                row = i * 128 + s if s < 128 else 512 + i * 64 + s - 128
                filtered[row : row + 16, n : n + 128] = total.astype(jnp.bfloat16)
    table_arriving.wait()

    def transform(row):
        return lax.dot_general(table[...], filtered[row : row + 256, :], NT, preferred_element_type=jnp.float32)

    def put(pair, lane, even, odd):
        rows = jnp.concatenate([even.reshape(CHAN // 8, 8, 128), odd.reshape(CHAN // 8, 8, 128)], axis=1)
        out_held[:, pair * 16 : pair * 16 + 16, lane : lane + 128] = rows.astype(jnp.bfloat16)

    for pair in range(2):
        product = transform(pair * 256)
        for p in range(2):
            part = product[p * CHAN : (p + 1) * CHAN]
            put(pair, p * 128, part[:, :128], part[:, 128:])
    product = transform(512)
    low = lax.broadcasted_iota(jnp.int32, (CHAN, 128), 1) < 64
    for pair in range(2):
        real = product[:CHAN, pair * 128 : (pair + 1) * 128]
        imag = product[CHAN:, pair * 128 : (pair + 1) * 128]
        put(
            pair, 256, jnp.where(low, real, pltpu.roll(imag, 64, 1)), jnp.where(low, pltpu.roll(real, 64, 1), imag)
        )
    leaving = pltpu.make_async_copy(out_held, out_ref, out_sem)
    leaving.start()
    leaving.wait()


def filter_section(samples, pfb_taps, table, first):
    in_hbm = pl.BlockSpec(memory_space=pltpu.HBM)
    return pl.pallas_call(
        functools.partial(spectra_kernel, first),
        in_specs=[in_hbm, in_hbm, pl.BlockSpec(memory_space=pltpu.VMEM)],
        out_specs=in_hbm,
        out_shape=pltpu.HBM((64, 32, LANES), jnp.bfloat16),
        scratch_shapes=[
            pltpu.VMEM((4, (HALF + TAPS - 1) * FRAME), jnp.bfloat16),
            pltpu.VMEM((2 * CHAN, FRAME), jnp.bfloat16),
            pltpu.VMEM((FRAME // 128, 4 * (HALF + 4), 128), jnp.float32),
            pltpu.VMEM((4 * HALF, FRAME), jnp.bfloat16),
            pltpu.VMEM((64, 32, LANES), jnp.bfloat16),
            pltpu.SemaphoreType.DMA,
            pltpu.SemaphoreType.DMA,
            pltpu.SemaphoreType.DMA,
        ],
        compiler_params=pltpu.CompilerParams(vmem_limit_bytes=40 * 1024 * 1024),
        name="filter_section",
    )(
        pltpu.with_memory_space_constraint(samples, pltpu.HBM),
        pltpu.with_memory_space_constraint(table, pltpu.HBM),
        pfb_taps,
    )


def reorder(order, source, out_ref, groups, row, lane):
    width = source.shape[-1]
    for g in range(groups):
        rows = source[g * 8 : (g + 1) * 8].reshape(256, width)
        turned = jnp.dot(order, rows, preferred_element_type=jnp.float32).astype(jnp.bfloat16)
        for c in range(8):
            out_ref[c, pl.ds(row + g * 32, 32), lane : lane + width] = turned[c * 32 : (c + 1) * 32]


def stacked(rows):
    low = lax.broadcasted_iota(jnp.int32, (rows.shape[0], 128), 1) < 64
    pieces = []
    for s in range(0, rows.shape[1], LANES):
        mixed = pltpu.roll(rows[:, s + 256 : s + 384].astype(jnp.float32), 64, 1)
        mixed = jnp.where(low, mixed, -mixed).astype(jnp.bfloat16)
        pieces += [rows[:, s + 128 : s + 256], -rows[:, s : s + 128], mixed]
    return jnp.concatenate([rows, jnp.concatenate(pieces, axis=1)], axis=0)


def self_kernel(order_ref, own0_ref, own1_ref, own_ref, self_ref, held):
    step = pl.program_id(0)

    @pl.when(step == 0)
    def _():
        reorder(order_ref[...], own0_ref, held, 8, 0, 0)
        reorder(order_ref[...], own1_ref, held, 8, 0, LANES)

    rows = held[step]
    own_ref[0] = rows
    product = lax.dot_general(stacked(rows), rows, NT, preferred_element_type=jnp.float32) * (1.0 / SPECTRA)
    self_ref[0, 0] = product[:BLOCK]
    self_ref[1, 0] = product[BLOCK:]


def self_tiles(order, own0, own1):
    whole = lambda a: pl.BlockSpec(a.shape, lambda c: (0,) * a.ndim)
    return pl.pallas_call(
        self_kernel,
        grid=(8,),
        in_specs=[whole(order), whole(own0), whole(own1)],
        out_specs=[
            pl.BlockSpec((1, BLOCK, 2 * LANES), lambda c: (c, 0, 0)),
            pl.BlockSpec((2, 1, BLOCK, BLOCK), lambda c: (0, c, 0, 0)),
        ],
        out_shape=[
            jax.ShapeDtypeStruct((8, BLOCK, 2 * LANES), jnp.bfloat16),
            jax.ShapeDtypeStruct((2, 8, BLOCK, BLOCK), jnp.float32),
        ],
        scratch_shapes=[pltpu.VMEM((8, BLOCK, 2 * LANES), jnp.bfloat16)],
        compiler_params=pltpu.CompilerParams(vmem_limit_bytes=40 * 1024 * 1024),
        name="self_tiles",
    )(order, own0, own1)


def columns(place_ref, order, f_ref, g_ref, h_ref, s_ref, out_ref):
    chip = place_ref[0]

    @pl.when(place_ref[1] == 0)
    def _():
        reorder(order, f_ref, out_ref, 4, pl.multiple_of(chip * 128, 128), 0)
        reorder(order, g_ref, out_ref, 4, pl.multiple_of((1 - chip) * 128, 128), 0)

    @pl.when(place_ref[1] == 1)
    def _():
        reorder(order, h_ref, out_ref, 8, 0, 0)

    reorder(order, s_ref, out_ref, 4, BLOCK, 0)


def early_kernel(place_ref, order_ref, f_ref, g_ref, h_ref, s_ref, out_ref):
    columns(place_ref, order_ref[...], f_ref, g_ref, h_ref, s_ref, out_ref)


SMALL = pl.BlockSpec(memory_space=pltpu.SMEM)
IN_VMEM = pl.BlockSpec(memory_space=pltpu.VMEM)


def early_columns(place, order, *received):
    return pl.pallas_call(
        early_kernel,
        in_specs=[SMALL] + [IN_VMEM] * 5,
        out_specs=IN_VMEM,
        out_shape=jax.ShapeDtypeStruct((8, BLOCK + BLOCK // 2, LANES), jnp.bfloat16),
        compiler_params=pltpu.CompilerParams(vmem_limit_bytes=40 * 1024 * 1024),
        name="early_columns",
    )(place, order, *received)


def cross_kernel(place_ref, order_ref, own_ref, early_ref, f_ref, g_ref, h_ref, s_ref, prior_ref, far_ref, held):
    step = pl.program_id(0)

    @pl.when(step == 0)
    def _():
        columns(place_ref, order_ref[...], f_ref, g_ref, h_ref, s_ref, held)

    cols = jnp.concatenate([early_ref[0], held[step]], axis=1)
    product = lax.dot_general(stacked(own_ref[0]), cols, NT, preferred_element_type=jnp.float32) * (1.0 / SPECTRA)
    prior_ref[0, 0] = product[:BLOCK, :BLOCK]
    prior_ref[1, 0] = product[BLOCK:, :BLOCK]
    far_ref[0, 0] = product[:BLOCK, BLOCK:]
    far_ref[1, 0] = product[BLOCK:, BLOCK:]


def cross_tiles(place, order, own, early, *late):
    whole = lambda a: pl.BlockSpec(a.shape, lambda c: (0,) * a.ndim)
    channel = lambda a: pl.BlockSpec((1,) + a.shape[1:], lambda c: (c, 0, 0))
    return pl.pallas_call(
        cross_kernel,
        grid=(8,),
        in_specs=[SMALL, whole(order), channel(own), channel(early)] + [whole(a) for a in late],
        out_specs=[
            pl.BlockSpec((2, 1, BLOCK, BLOCK), lambda c: (0, c, 0, 0)),
            pl.BlockSpec((2, 1, BLOCK, BLOCK // 2), lambda c: (0, c, 0, 0)),
        ],
        out_shape=[
            jax.ShapeDtypeStruct((2, 8, BLOCK, BLOCK), jnp.float32),
            jax.ShapeDtypeStruct((2, 8, BLOCK, BLOCK // 2), jnp.float32),
        ],
        scratch_shapes=[pltpu.VMEM((8, BLOCK + BLOCK // 2, LANES), jnp.bfloat16)],
        compiler_params=pltpu.CompilerParams(vmem_limit_bytes=48 * 1024 * 1024),
        name="cross_tiles",
    )(place, order, own, early, *late)


CROSSED = [(0, 3), (1, 2), (2, 1), (3, 0)]
ODD_OVER = [(1, 2), (3, 0)]
EVEN_UP = [(0, 1), (2, 3)]
SWAPPED = [(0, 1), (1, 0), (2, 3), (3, 2)]


def on_device(table, order, samples, pfb_taps):
    position = lax.axis_index("narrow")
    chip = position // 2
    place = jnp.stack([chip, position % 2]).astype(jnp.int32)

    def turn(chunk):
        return lax.all_to_all(chunk, "wide", split_axis=0, concat_axis=0, tiled=True)

    def halves(own):
        shape = (32,) + own.shape[1:]
        return tuple(lax.dynamic_slice(own, (start * 32, 0, 0), shape) for start in (1 - chip, chip))

    def exchange(own, crossing, rest):
        f = lax.ppermute(crossing, "narrow", CROSSED)
        g = lax.ppermute(rest, "narrow", ODD_OVER)
        h = lax.ppermute(own, "narrow", EVEN_UP)
        return f, g, h

    def swap(f):
        return lax.ppermute(f, "narrow", SWAPPED)

    early = filter_section(samples, pfb_taps, table, 0)
    late = filter_section(samples, pfb_taps, table, HALF)
    own0 = turn(early)
    late, own0 = lax.optimization_barrier((late, own0))
    own1 = turn(late)
    received = exchange(own0, *halves(own0))
    held0 = early_columns(place, order, *received, swap(received[0]))
    own1, held0 = lax.optimization_barrier((own1, held0))
    crossing, rest = halves(own1)
    f, g, h = exchange(own1, crossing, rest)
    own1, crossing, rest = lax.optimization_barrier((own1, crossing, rest))
    mine, self_vis = self_tiles(order, own0, own1)
    f, mine = lax.optimization_barrier((f, mine))
    prior_vis, far_vis = cross_tiles(place, order, mine, held0, f, g, h, swap(f))
    return (self_vis, prior_vis, far_vis)


def solution(mesh):
    return jax.shard_map(
        functools.partial(on_device, dft_table(), row_order()),
        mesh=mesh,
        in_specs=(P(("narrow", "wide"), None), P()),
        out_specs=(
            P(None, "wide", "narrow", None),
            P(None, "wide", "narrow", None),
            P(None, "wide", "narrow", None),
        ),
        check_vma=False,
    )
```

```python
import functools
import math

import jax
import jax.numpy as jnp
import numpy as np
from jax import lax
from jax.experimental import pallas as pl
from jax.experimental.pallas import tpu as pltpu
from jax.sharding import Mesh
from jax.sharding import PartitionSpec as P

CHAN = 512
TAPS = 4
SPECTRA = 384
BLOCK = 256
FRAME = 2 * CHAN
HALF = SPECTRA // 2
LANES = 2 * HALF
NT = (((1,), (1,)), ((), ()))
SMALL = pl.BlockSpec(memory_space=pltpu.SMEM)
IN_VMEM = pl.BlockSpec(memory_space=pltpu.VMEM)


def dft_table():
    positions = np.arange(FRAME, dtype=np.int32)
    bins = np.arange(CHAN, dtype=np.int32)
    phases = bins[:, None] * positions[None, :] % FRAME
    angles = phases.astype(np.float32) * np.float32(math.pi / CHAN)
    norming = np.float32(FRAME ** (-0.5))
    table = np.concatenate([np.cos(angles) * norming, -np.sin(angles) * norming])
    return table.astype(jnp.bfloat16)


def row_order():
    order = np.arange(256).reshape(32, 8).T.reshape(-1)
    return np.eye(256, dtype=np.float32)[order].astype(jnp.bfloat16)


PIECES = 3


def spectra_kernel(first, split, place_ref, x_ref, table_ref, taps_ref, *refs):
    outs, (x_held, table, taps_held, frames, filtered, out_held, x_sem, table_sem, taps_sem, out_sem) = refs[:-10], refs[-10:]
    step = (HALF + TAPS - 1) // PIECES
    arriving = [
        pltpu.make_async_copy(
            x_ref.at[:, pl.ds((first + j * step) * FRAME, step * FRAME)], x_held.at[j], x_sem.at[j]
        )
        for j in range(PIECES)
    ]
    table_arriving = pltpu.make_async_copy(table_ref, table, table_sem)
    taps_arriving = pltpu.make_async_copy(taps_ref, taps_held, taps_sem)
    arriving[0].start()
    taps_arriving.start()
    for copy in arriving[1:]:
        copy.start()
    table_arriving.start()
    for j in range(PIECES):
        arriving[j].wait()
        for f in range(step):
            for n in range(0, FRAME, 128):
                frames[n // 128, 4 * (j * step + f) : 4 * (j * step + f) + 4, :] = x_held[
                    j, :, f * FRAME + n : f * FRAME + n + 128
                ].astype(jnp.float32)
    taps_arriving.wait()
    for n in range(0, FRAME, 128):
        taps = [taps_held[t : t + 1, n : n + 128] for t in range(TAPS)]
        for i in range(4):
            for s in range(0, HALF, 16):
                total = frames[n // 128, pl.ds(i + 4 * s, 16, stride=4), :] * taps[0]
                for t in range(1, TAPS):
                    total = total + frames[n // 128, pl.ds(i + 4 * (s + t), 16, stride=4), :] * taps[t]
                row = i * 128 + s if s < 128 else 512 + i * 64 + s - 128
                filtered[row : row + 16, n : n + 128] = total.astype(jnp.bfloat16)
    table_arriving.wait()

    def transform(row):
        return lax.dot_general(table[...], filtered[row : row + 256, :], NT, preferred_element_type=jnp.float32)

    def put(pair, lane, even, odd):
        rows = jnp.concatenate([even.reshape(CHAN // 8, 8, 128), odd.reshape(CHAN // 8, 8, 128)], axis=1)
        out_held[:, pair * 16 : pair * 16 + 16, lane : lane + 128] = rows.astype(jnp.bfloat16)

    for pair in range(2):
        product = transform(pair * 256)
        for p in range(2):
            part = product[p * CHAN : (p + 1) * CHAN]
            put(pair, p * 128, part[:, :128], part[:, 128:])
    product = transform(512)
    low = lax.broadcasted_iota(jnp.int32, (CHAN, 128), 1) < 64
    for pair in range(2):
        real = product[:CHAN, pair * 128 : (pair + 1) * 128]
        imag = product[CHAN:, pair * 128 : (pair + 1) * 128]
        put(
            pair, 256, jnp.where(low, real, pltpu.roll(imag, 64, 1)), jnp.where(low, pltpu.roll(real, 64, 1), imag)
        )
    if split:
        side = place_ref[2]
        sources = [out_held.at[pl.ds(side * 32, 32)], out_held.at[pl.ds((1 - side) * 32, 32)]]
    else:
        sources = [out_held]
    leaving = [pltpu.make_async_copy(source, out, out_sem.at[j]) for j, (source, out) in enumerate(zip(sources, outs))]
    for copy in leaving:
        copy.start()
    for copy in leaving:
        copy.wait()


def filter_section(place, samples, pfb_taps, table, first, split):
    in_hbm = pl.BlockSpec(memory_space=pltpu.HBM)
    out_shape = [pltpu.HBM((32, 32, LANES), jnp.bfloat16)] * 2 if split else [pltpu.HBM((64, 32, LANES), jnp.bfloat16)]
    return pl.pallas_call(
        functools.partial(spectra_kernel, first, split),
        in_specs=[SMALL, in_hbm, in_hbm, in_hbm],
        out_specs=[in_hbm] * len(out_shape),
        out_shape=out_shape,
        scratch_shapes=[
            pltpu.VMEM((PIECES, 4, (HALF + TAPS - 1) // PIECES * FRAME), jnp.bfloat16),
            pltpu.VMEM((2 * CHAN, FRAME), jnp.bfloat16),
            pltpu.VMEM((TAPS, FRAME), jnp.float32),
            pltpu.VMEM((FRAME // 128, 4 * (HALF + 4), 128), jnp.float32),
            pltpu.VMEM((4 * HALF, FRAME), jnp.bfloat16),
            pltpu.VMEM((64, 32, LANES), jnp.bfloat16),
            pltpu.SemaphoreType.DMA((PIECES,)),
            pltpu.SemaphoreType.DMA,
            pltpu.SemaphoreType.DMA,
            pltpu.SemaphoreType.DMA((2,)),
        ],
        compiler_params=pltpu.CompilerParams(vmem_limit_bytes=40 * 1024 * 1024),
        name="filter_section",
    )(place, *(pltpu.with_memory_space_constraint(a, pltpu.HBM) for a in (samples, table, pfb_taps)))


def merge_kernel(place_ref, stay_ref, got_ref, out_ref, sem):
    side = place_ref[2]
    copies = [
        pltpu.make_async_copy(stay_ref, out_ref.at[:, side], sem.at[0]),
        pltpu.make_async_copy(got_ref, out_ref.at[:, 1 - side], sem.at[1]),
    ]
    for copy in copies:
        copy.start()
    for copy in copies:
        copy.wait()


def merge(place, stay, got):
    in_hbm = pl.BlockSpec(memory_space=pltpu.HBM)
    return pl.pallas_call(
        merge_kernel,
        in_specs=[SMALL, in_hbm, in_hbm],
        out_specs=in_hbm,
        out_shape=pltpu.HBM((32, 2, 32, LANES), jnp.bfloat16),
        scratch_shapes=[pltpu.SemaphoreType.DMA((2,))],
        name="merge_sides",
    )(place, *(pltpu.with_memory_space_constraint(a, pltpu.HBM) for a in (stay, got)))


def rows_kernel(place_ref, order_ref, source_ref, cross_ref, rest_ref, whole_ref):
    chip = place_ref[0]
    order = order_ref[...]
    for out_ref, half in ((cross_ref, 1 - chip), (rest_ref, chip)):
        for g in range(4):
            if len(source_ref.shape) == 3:
                rows = source_ref[pl.ds(half * 32 + g * 8, 8)]
            else:
                rows = source_ref[g * 8 : (g + 1) * 8, half]
            turned = jnp.dot(order, rows.reshape(256, LANES), preferred_element_type=jnp.float32).astype(jnp.bfloat16)
            for c in range(8):
                part = turned[c * 32 : (c + 1) * 32]
                out_ref[c, g * 32 : (g + 1) * 32, :] = part
                whole_ref[c, pl.ds(pl.multiple_of(half * 128 + g * 32, 32), 32), :] = part


def channel_rows(place, order, source):
    shapes = [(8, 128, LANES), (8, 128, LANES), (8, BLOCK, LANES)]
    return pl.pallas_call(
        rows_kernel,
        in_specs=[SMALL, IN_VMEM, IN_VMEM],
        out_specs=[IN_VMEM] * 3,
        out_shape=[jax.ShapeDtypeStruct(shape, jnp.bfloat16) for shape in shapes],
        compiler_params=pltpu.CompilerParams(vmem_limit_bytes=40 * 1024 * 1024),
        name="channel_rows",
    )(place, order, source)


def stacked(rows):
    low = lax.broadcasted_iota(jnp.int32, (rows.shape[0], 128), 1) < 64
    pieces = []
    for s in range(0, rows.shape[1], LANES):
        mixed = pltpu.roll(rows[:, s + 256 : s + 384].astype(jnp.float32), 64, 1)
        mixed = jnp.where(low, mixed, -mixed).astype(jnp.bfloat16)
        pieces += [rows[:, s + 128 : s + 256], -rows[:, s : s + 128], mixed]
    return jnp.concatenate([rows, jnp.concatenate(pieces, axis=1)], axis=0)


def tile_products(rows, cols):
    return lax.dot_general(stacked(rows), cols, NT, preferred_element_type=jnp.float32) * (1.0 / SPECTRA)


def self_kernel(own0_ref, own1_ref, self_ref, self_held, sem):
    copies = []
    for c in range(8):
        rows = jnp.concatenate([own0_ref[c], own1_ref[c]], axis=1)
        product = tile_products(rows, rows)
        self_held[0, c] = product[:BLOCK]
        self_held[1, c] = product[BLOCK:]
        copies.append(pltpu.make_async_copy(self_held.at[:, c], self_ref.at[:, c], sem.at[c]))
        copies[-1].start()
    for copy in copies:
        copy.wait()


def self_tiles(own0, own1):
    return pl.pallas_call(
        self_kernel,
        in_specs=[IN_VMEM] * 2,
        out_specs=pl.BlockSpec(memory_space=pltpu.HBM),
        out_shape=pltpu.HBM((2, 8, BLOCK, BLOCK), jnp.float32),
        scratch_shapes=[pltpu.VMEM((2, 8, BLOCK, BLOCK), jnp.float32), pltpu.SemaphoreType.DMA((8,))],
        compiler_params=pltpu.CompilerParams(vmem_limit_bytes=40 * 1024 * 1024),
        name="self_tiles",
    )(own0, own1)


def put_columns(place_ref, f_ref, g_ref, h_ref, s_ref, out_ref, lane):
    chip = place_ref[0]
    lanes = slice(lane, lane + LANES)

    @pl.when(place_ref[1] == 0)
    def _():
        out_ref[:, pl.ds(pl.multiple_of(chip * 128, 128), 128), lanes] = f_ref[...]
        out_ref[:, pl.ds(pl.multiple_of((1 - chip) * 128, 128), 128), lanes] = g_ref[...]

    @pl.when(place_ref[1] == 1)
    def _():
        out_ref[:, :BLOCK, lanes] = h_ref[...]

    out_ref[:, BLOCK:, lanes] = s_ref[...]


def early_kernel(place_ref, f_ref, g_ref, h_ref, s_ref, out_ref):
    put_columns(place_ref, f_ref, g_ref, h_ref, s_ref, out_ref, 0)


def early_columns(place, *received):
    return pl.pallas_call(
        early_kernel,
        in_specs=[SMALL] + [IN_VMEM] * 4,
        out_specs=IN_VMEM,
        out_shape=jax.ShapeDtypeStruct((8, BLOCK + BLOCK // 2, LANES), jnp.bfloat16),
        compiler_params=pltpu.CompilerParams(vmem_limit_bytes=40 * 1024 * 1024),
        name="early_columns",
    )(place, *received)


def cross_kernel(place_ref, own0_ref, own1_ref, early_ref, f_ref, g_ref, h_ref, s_ref, prior_ref, far_ref,
                 held, prior_held, far_held, prior_sem, far_sem):
    put_columns(place_ref, f_ref, g_ref, h_ref, s_ref, held, 0)
    copies = []
    for c in range(8):
        rows = jnp.concatenate([own0_ref[c], own1_ref[c]], axis=1)
        product = tile_products(rows, jnp.concatenate([early_ref[c], held[c]], axis=1))
        for p in range(2):
            prior_held[p, c] = product[p * BLOCK : (p + 1) * BLOCK, :BLOCK]
            far_held[p, c] = product[p * BLOCK : (p + 1) * BLOCK, BLOCK:]
        copies.append(pltpu.make_async_copy(prior_held.at[:, c], prior_ref.at[:, c], prior_sem.at[c]))
        copies.append(pltpu.make_async_copy(far_held.at[:, c], far_ref.at[:, c], far_sem.at[c]))
        copies[-2].start()
        copies[-1].start()
    for copy in copies:
        copy.wait()


def cross_tiles(place, own0, own1, early, *late):
    in_hbm = pl.BlockSpec(memory_space=pltpu.HBM)
    prior_shape, far_shape = (2, 8, BLOCK, BLOCK), (2, 8, BLOCK, BLOCK // 2)
    return pl.pallas_call(
        cross_kernel,
        in_specs=[SMALL] + [IN_VMEM] * (3 + len(late)),
        out_specs=[in_hbm, in_hbm],
        out_shape=[pltpu.HBM(prior_shape, jnp.float32), pltpu.HBM(far_shape, jnp.float32)],
        scratch_shapes=[
            pltpu.VMEM((8, BLOCK + BLOCK // 2, LANES), jnp.bfloat16),
            pltpu.VMEM(prior_shape, jnp.float32),
            pltpu.VMEM(far_shape, jnp.float32),
            pltpu.SemaphoreType.DMA((8,)),
            pltpu.SemaphoreType.DMA((8,)),
        ],
        compiler_params=pltpu.CompilerParams(vmem_limit_bytes=40 * 1024 * 1024),
        name="cross_tiles",
    )(place, own0, own1, early, *late)


CROSSED = [(0, 3), (1, 2), (2, 1), (3, 0)]
ODD_OVER = [(1, 2), (3, 0)]
EVEN_UP = [(0, 1), (2, 3)]
SWAPPED = [(0, 1), (1, 0), (2, 3), (3, 2)]


def on_device(table, order, samples, pfb_taps):
    position = lax.axis_index("narrow")
    place = jnp.stack([position // 2, position % 2, lax.axis_index("side")]).astype(jnp.int32)

    def exchange(crossing, rest, whole):
        f = lax.ppermute(crossing, "narrow", CROSSED)
        g = lax.ppermute(rest, "narrow", ODD_OVER)
        h = lax.ppermute(whole, "narrow", EVEN_UP)
        return f, g, h

    def swap(f):
        return lax.ppermute(f, "narrow", SWAPPED)

    (early,) = filter_section(place, samples, pfb_taps, table, 0, False)
    stay, leave = filter_section(place, samples, pfb_taps, table, HALF, True)
    source0 = lax.all_to_all(early, ("side", "plane"), split_axis=0, concat_axis=0, tiled=True)
    late = merge(place, stay, lax.ppermute(leave, "side", [(0, 1), (1, 0)]))
    late, source0 = lax.optimization_barrier((late, source0))
    source1 = lax.all_to_all(late, "plane", split_axis=0, concat_axis=0, tiled=True)
    crossing0, rest0, own0 = channel_rows(place, order, source0)
    f, g, h = exchange(crossing0, rest0, own0)
    held0 = early_columns(place, f, g, h, swap(f))
    source1, held0 = lax.optimization_barrier((source1, held0))
    crossing1, rest1, own1 = channel_rows(place, order, source1)
    f, g, h = exchange(crossing1, rest1, own1)
    self_vis = self_tiles(own0, own1)
    f, self_vis = lax.optimization_barrier((f, self_vis))
    prior_vis, far_vis = cross_tiles(place, own0, own1, held0, f, g, h, swap(f))
    return (self_vis, prior_vis, far_vis)


def solution(mesh):
    parted = Mesh(mesh.devices.reshape(2, mesh.devices.shape[0] // 2, mesh.devices.shape[1]), ("side", "plane", "narrow"))
    out_spec = P(None, ("side", "plane"), "narrow", None)
    return jax.shard_map(
        functools.partial(on_device, dft_table(), row_order()),
        mesh=parted,
        in_specs=(P(("narrow", "side", "plane"), None), P()),
        out_specs=(out_spec, out_spec, out_spec),
        check_vma=False,
    )
```

```python
import functools
import math

import jax
import jax.numpy as jnp
import numpy as np
from jax import lax
from jax.experimental import pallas as pl
from jax.experimental.pallas import tpu as pltpu
from jax.sharding import Mesh
from jax.sharding import PartitionSpec as P

CHAN = 512
TAPS = 4
SPECTRA = 384
BLOCK = 256
FRAME = 2 * CHAN
SB = 128
EARLY = 2
NT = (((1,), (1,)), ((), ()))
SMALL = pl.BlockSpec(memory_space=pltpu.SMEM)
IN_VMEM = pl.BlockSpec(memory_space=pltpu.VMEM)


def dft_table():
    positions = np.arange(FRAME, dtype=np.int32)
    bins = np.arange(CHAN, dtype=np.int32)
    phases = bins[:, None] * positions[None, :] % FRAME
    angles = phases.astype(np.float32) * np.float32(math.pi / CHAN)
    norming = np.float32(FRAME ** (-0.5))
    table = np.concatenate([np.cos(angles) * norming, -np.sin(angles) * norming])
    return table.astype(jnp.bfloat16)


def row_order():
    order = np.arange(256).reshape(32, 8).T.reshape(-1)
    return np.eye(256, dtype=np.float32)[order].astype(jnp.bfloat16)


def spectra_kernel(first, split, place_ref, x_ref, table_ref, taps_ref, *refs):
    outs, (x_held, table, taps_held, frames, filtered, out_held, x_sem, table_sem, taps_sem, out_sem) = refs[:-10], refs[-10:]
    blocks = x_held.shape[0]
    extra = TAPS - 1
    arriving = []
    for j in range(blocks):
        start, length = (first, SB + extra) if j == 0 else (first + j * SB + extra, SB)
        arriving.append(
            pltpu.make_async_copy(
                x_ref.at[:, pl.ds(start * FRAME, length * FRAME)], x_held.at[j, :, pl.ds(0, length * FRAME)], x_sem.at[j]
            )
        )
    table_arriving = pltpu.make_async_copy(table_ref, table, table_sem)
    taps_arriving = pltpu.make_async_copy(taps_ref, taps_held, taps_sem)
    taps_arriving.start()
    arriving[0].start()
    table_arriving.start()
    for copy in arriving[1:]:
        copy.start()
    taps_arriving.wait()
    leaving = []
    for j in range(blocks):
        arriving[j].wait()
        start, length = (0, SB + extra) if j == 0 else (j * SB + extra, SB)
        for f in range(length):
            for n in range(0, FRAME, 128):
                frames[n // 128, 4 * (start + f) : 4 * (start + f) + 4, :] = x_held[
                    j, :, f * FRAME + n : f * FRAME + n + 128
                ].astype(jnp.float32)
        for n in range(0, FRAME, 128):
            taps = [taps_held[t : t + 1, n : n + 128] for t in range(TAPS)]
            for i in range(4):
                for s in range(j * SB, (j + 1) * SB, 16):
                    total = frames[n // 128, pl.ds(i + 4 * s, 16, stride=4), :] * taps[0]
                    for t in range(1, TAPS):
                        total = total + frames[n // 128, pl.ds(i + 4 * (s + t), 16, stride=4), :] * taps[t]
                    row = i * SB + s - j * SB
                    filtered[row : row + 16, n : n + 128] = total.astype(jnp.bfloat16)
        if j == 0:
            table_arriving.wait()
        for pair in range(2):
            product = lax.dot_general(
                table[...], filtered[pair * 2 * SB : (pair + 1) * 2 * SB, :], NT, preferred_element_type=jnp.float32
            )
            for p in range(2):
                part = product[p * CHAN : (p + 1) * CHAN]
                rows = jnp.concatenate(
                    [part[:, :SB].reshape(CHAN // 8, 8, SB), part[:, SB:].reshape(CHAN // 8, 8, SB)], axis=1
                )
                out_held[j, :, pair * 16 : pair * 16 + 16, p * SB : (p + 1) * SB] = rows.astype(jnp.bfloat16)
        if split:
            side = place_ref[2]
            sources = [out_held.at[j, pl.ds(side * 32, 32)], out_held.at[j, pl.ds((1 - side) * 32, 32)]]
        else:
            sources = [out_held.at[j]]
        for k, (source, out) in enumerate(zip(sources, outs)):
            copy = pltpu.make_async_copy(source, out.at[:, :, pl.ds(j * 2 * SB, 2 * SB)], out_sem.at[2 * j + k])
            copy.start()
            leaving.append(copy)
    for copy in leaving:
        copy.wait()


def filter_section(place, samples, pfb_taps, table, first, blocks, split):
    in_hbm = pl.BlockSpec(memory_space=pltpu.HBM)
    lanes = blocks * 2 * SB
    out_shape = [pltpu.HBM((32, 32, lanes), jnp.bfloat16)] * 2 if split else [pltpu.HBM((64, 32, lanes), jnp.bfloat16)]
    return pl.pallas_call(
        functools.partial(spectra_kernel, first, split),
        in_specs=[SMALL, in_hbm, in_hbm, in_hbm],
        out_specs=[in_hbm] * len(out_shape),
        out_shape=out_shape,
        scratch_shapes=[
            pltpu.VMEM((blocks, 4, (SB + TAPS - 1) * FRAME), jnp.bfloat16),
            pltpu.VMEM((2 * CHAN, FRAME), jnp.bfloat16),
            pltpu.VMEM((TAPS, FRAME), jnp.float32),
            pltpu.VMEM((FRAME // 128, 4 * (blocks * SB + 4), 128), jnp.float32),
            pltpu.VMEM((4 * SB, FRAME), jnp.bfloat16),
            pltpu.VMEM((blocks, 64, 32, 2 * SB), jnp.bfloat16),
            pltpu.SemaphoreType.DMA((blocks,)),
            pltpu.SemaphoreType.DMA,
            pltpu.SemaphoreType.DMA,
            pltpu.SemaphoreType.DMA((2 * blocks,)),
        ],
        compiler_params=pltpu.CompilerParams(vmem_limit_bytes=40 * 1024 * 1024),
        name="filter_section",
    )(place, *(pltpu.with_memory_space_constraint(a, pltpu.HBM) for a in (samples, table, pfb_taps)))


def merge_kernel(place_ref, stay_ref, got_ref, out_ref, held, sem):
    side = place_ref[2]
    held[:, side] = stay_ref[...]
    held[:, 1 - side] = got_ref[...]
    copy = pltpu.make_async_copy(held, out_ref, sem)
    copy.start()
    copy.wait()


def merge(place, stay, got):
    shape = (32, 2) + stay.shape[1:]
    return pl.pallas_call(
        merge_kernel,
        in_specs=[SMALL, IN_VMEM, IN_VMEM],
        out_specs=pl.BlockSpec(memory_space=pltpu.HBM),
        out_shape=pltpu.HBM(shape, jnp.bfloat16),
        scratch_shapes=[pltpu.VMEM(shape, jnp.bfloat16), pltpu.SemaphoreType.DMA],
        compiler_params=pltpu.CompilerParams(vmem_limit_bytes=40 * 1024 * 1024),
        name="merge_sides",
    )(place, stay, got)


def rows_kernel(place_ref, order_ref, source_ref, cross_ref, rest_ref, whole_ref):
    chip = place_ref[0]
    order = order_ref[...]
    for out_ref, half in ((cross_ref, 1 - chip), (rest_ref, chip)):
        for g in range(4):
            if len(source_ref.shape) == 3:
                rows = source_ref[pl.ds(half * 32 + g * 8, 8)]
            else:
                rows = source_ref[g * 8 : (g + 1) * 8, half]
            turned = jnp.dot(order, rows.reshape(256, rows.shape[-1]), preferred_element_type=jnp.float32).astype(jnp.bfloat16)
            for c in range(8):
                part = turned[c * 32 : (c + 1) * 32]
                out_ref[c, g * 32 : (g + 1) * 32, :] = part
                whole_ref[c, pl.ds(pl.multiple_of(half * 128 + g * 32, 32), 32), :] = part


def channel_rows(place, order, source):
    lanes = source.shape[-1]
    shapes = [(8, 128, lanes), (8, 128, lanes), (8, BLOCK, lanes)]
    return pl.pallas_call(
        rows_kernel,
        in_specs=[SMALL, IN_VMEM, IN_VMEM],
        out_specs=[IN_VMEM] * 3,
        out_shape=[jax.ShapeDtypeStruct(shape, jnp.bfloat16) for shape in shapes],
        compiler_params=pltpu.CompilerParams(vmem_limit_bytes=40 * 1024 * 1024),
        name="channel_rows",
    )(place, order, source)


def stacked(rows):
    pieces = []
    for s in range(0, rows.shape[1], 2 * SB):
        pieces += [rows[:, s + SB : s + 2 * SB], -rows[:, s : s + SB]]
    return jnp.concatenate([rows, jnp.concatenate(pieces, axis=1)], axis=0)


def tile_products(rows, cols):
    return lax.dot_general(stacked(rows), cols, NT, preferred_element_type=jnp.float32) * (1.0 / SPECTRA)


def self_kernel(own0_ref, own1_ref, self_ref, self_held, sem):
    copies = []
    for c in range(8):
        rows = jnp.concatenate([own0_ref[c], own1_ref[c]], axis=1)
        product = tile_products(rows, rows)
        self_held[0, c] = product[:BLOCK]
        self_held[1, c] = product[BLOCK:]
        copies.append(pltpu.make_async_copy(self_held.at[:, c], self_ref.at[:, c], sem.at[c]))
        copies[-1].start()
    for copy in copies:
        copy.wait()


def self_tiles(own0, own1):
    return pl.pallas_call(
        self_kernel,
        in_specs=[IN_VMEM] * 2,
        out_specs=pl.BlockSpec(memory_space=pltpu.HBM),
        out_shape=pltpu.HBM((2, 8, BLOCK, BLOCK), jnp.float32),
        scratch_shapes=[pltpu.VMEM((2, 8, BLOCK, BLOCK), jnp.float32), pltpu.SemaphoreType.DMA((8,))],
        compiler_params=pltpu.CompilerParams(vmem_limit_bytes=40 * 1024 * 1024),
        name="self_tiles",
    )(own0, own1)


def put_columns(place_ref, f_ref, g_ref, h_ref, s_ref, out_ref):
    chip = place_ref[0]

    @pl.when(place_ref[1] == 0)
    def _():
        out_ref[:, pl.ds(pl.multiple_of(chip * 128, 128), 128), :] = f_ref[...]
        out_ref[:, pl.ds(pl.multiple_of((1 - chip) * 128, 128), 128), :] = g_ref[...]

    @pl.when(place_ref[1] == 1)
    def _():
        out_ref[:, :BLOCK, :] = h_ref[...]

    out_ref[:, BLOCK:, :] = s_ref[...]


def early_kernel(place_ref, f_ref, g_ref, h_ref, s_ref, out_ref):
    put_columns(place_ref, f_ref, g_ref, h_ref, s_ref, out_ref)


def early_columns(place, *received):
    return pl.pallas_call(
        early_kernel,
        in_specs=[SMALL] + [IN_VMEM] * 4,
        out_specs=IN_VMEM,
        out_shape=jax.ShapeDtypeStruct((8, BLOCK + BLOCK // 2, received[0].shape[-1]), jnp.bfloat16),
        compiler_params=pltpu.CompilerParams(vmem_limit_bytes=40 * 1024 * 1024),
        name="early_columns",
    )(place, *received)


def cross_kernel(place_ref, own0_ref, own1_ref, early_ref, f_ref, g_ref, h_ref, s_ref, prior_ref, far_ref,
                 held, prior_held, far_held, prior_sem, far_sem):
    put_columns(place_ref, f_ref, g_ref, h_ref, s_ref, held)
    copies = []
    for c in range(8):
        rows = jnp.concatenate([own0_ref[c], own1_ref[c]], axis=1)
        product = tile_products(rows, jnp.concatenate([early_ref[c], held[c]], axis=1))
        for p in range(2):
            prior_held[p, c] = product[p * BLOCK : (p + 1) * BLOCK, :BLOCK]
            far_held[p, c] = product[p * BLOCK : (p + 1) * BLOCK, BLOCK:]
        copies.append(pltpu.make_async_copy(prior_held.at[:, c], prior_ref.at[:, c], prior_sem.at[c]))
        copies.append(pltpu.make_async_copy(far_held.at[:, c], far_ref.at[:, c], far_sem.at[c]))
        copies[-2].start()
        copies[-1].start()
    for copy in copies:
        copy.wait()


def cross_tiles(place, own0, own1, early, *late):
    in_hbm = pl.BlockSpec(memory_space=pltpu.HBM)
    prior_shape, far_shape = (2, 8, BLOCK, BLOCK), (2, 8, BLOCK, BLOCK // 2)
    return pl.pallas_call(
        cross_kernel,
        in_specs=[SMALL] + [IN_VMEM] * (3 + len(late)),
        out_specs=[in_hbm, in_hbm],
        out_shape=[pltpu.HBM(prior_shape, jnp.float32), pltpu.HBM(far_shape, jnp.float32)],
        scratch_shapes=[
            pltpu.VMEM((8, BLOCK + BLOCK // 2, late[0].shape[-1]), jnp.bfloat16),
            pltpu.VMEM(prior_shape, jnp.float32),
            pltpu.VMEM(far_shape, jnp.float32),
            pltpu.SemaphoreType.DMA((8,)),
            pltpu.SemaphoreType.DMA((8,)),
        ],
        compiler_params=pltpu.CompilerParams(vmem_limit_bytes=40 * 1024 * 1024),
        name="cross_tiles",
    )(place, own0, own1, early, *late)


CROSSED = [(0, 3), (1, 2), (2, 1), (3, 0)]
ODD_OVER = [(1, 2), (3, 0)]
EVEN_UP = [(0, 1), (2, 3)]
SWAPPED = [(0, 1), (1, 0), (2, 3), (3, 2)]


def on_device(table, order, samples, pfb_taps):
    position = lax.axis_index("narrow")
    place = jnp.stack([position // 2, position % 2, lax.axis_index("side")]).astype(jnp.int32)

    def exchange(crossing, rest, whole):
        f = lax.ppermute(crossing, "narrow", CROSSED)
        g = lax.ppermute(rest, "narrow", ODD_OVER)
        h = lax.ppermute(whole, "narrow", EVEN_UP)
        return f, g, h

    def swap(f):
        return lax.ppermute(f, "narrow", SWAPPED)

    (early,) = filter_section(place, samples, pfb_taps, table, 0, EARLY, False)
    stay, leave = filter_section(place, samples, pfb_taps, table, EARLY * SB, 1, True)
    source0 = lax.all_to_all(early, ("side", "plane"), split_axis=0, concat_axis=0, tiled=True)
    late = merge(place, stay, lax.ppermute(leave, "side", [(0, 1), (1, 0)]))
    late, source0 = lax.optimization_barrier((late, source0))
    source1 = lax.all_to_all(late, "plane", split_axis=0, concat_axis=0, tiled=True)
    crossing0, rest0, own0 = channel_rows(place, order, source0)
    f, g, h = exchange(crossing0, rest0, own0)
    held0 = early_columns(place, f, g, h, swap(f))
    source1, held0 = lax.optimization_barrier((source1, held0))
    crossing1, rest1, own1 = channel_rows(place, order, source1)
    f, g, h = exchange(crossing1, rest1, own1)
    own1, h = lax.optimization_barrier((own1, h))
    self_vis = self_tiles(own0, own1)
    f, self_vis = lax.optimization_barrier((f, self_vis))
    prior_vis, far_vis = cross_tiles(place, own0, own1, held0, f, g, h, swap(f))
    return (self_vis, prior_vis, far_vis)


def solution(mesh):
    parted = Mesh(mesh.devices.reshape(2, mesh.devices.shape[0] // 2, mesh.devices.shape[1]), ("side", "plane", "narrow"))
    out_spec = P(None, ("side", "plane"), "narrow", None)
    return jax.shard_map(
        functools.partial(on_device, dft_table(), row_order()),
        mesh=parted,
        in_specs=(P(("narrow", "side", "plane"), None), P()),
        out_specs=(out_spec, out_spec, out_spec),
        check_vma=False,
    )
```

```python
import functools
import math

import jax
import jax.numpy as jnp
import numpy as np
from jax import lax
from jax.experimental import pallas as pl
from jax.experimental.pallas import tpu as pltpu
from jax.sharding import Mesh
from jax.sharding import PartitionSpec as P

CHAN = 512
TAPS = 4
SPECTRA = 384
BLOCK = 256
FRAME = 2 * CHAN
SB = 128
EARLY = 2
NT = (((1,), (1,)), ((), ()))
SMALL = pl.BlockSpec(memory_space=pltpu.SMEM)
IN_VMEM = pl.BlockSpec(memory_space=pltpu.VMEM)


def dft_table():
    positions = np.arange(FRAME, dtype=np.int32)
    bins = np.arange(CHAN, dtype=np.int32)
    phases = bins[:, None] * positions[None, :] % FRAME
    angles = phases.astype(np.float32) * np.float32(math.pi / CHAN)
    norming = np.float32(FRAME ** (-0.5))
    table = np.concatenate([np.cos(angles) * norming, -np.sin(angles) * norming])
    return table.astype(jnp.bfloat16)


def row_order():
    order = np.arange(256).reshape(32, 8).T.reshape(-1)
    return np.eye(256, dtype=np.float32)[order].astype(jnp.bfloat16)


def spectra_kernel(first, split, place_ref, x_ref, table_ref, taps_ref, *refs):
    outs, (x_held, table, taps_held, frames, filtered, out_held, x_sem, table_sem, taps_sem, out_sem) = refs[:-10], refs[-10:]
    blocks = x_held.shape[0]
    extra = TAPS - 1
    arriving = []
    for j in range(blocks):
        start, length = (first, SB + extra) if j == 0 else (first + j * SB + extra, SB)
        arriving.append(
            pltpu.make_async_copy(
                x_ref.at[:, pl.ds(start * FRAME, length * FRAME)], x_held.at[j, :, pl.ds(0, length * FRAME)], x_sem.at[j]
            )
        )
    table_arriving = pltpu.make_async_copy(table_ref, table, table_sem)
    taps_arriving = pltpu.make_async_copy(taps_ref, taps_held, taps_sem)
    taps_arriving.start()
    arriving[0].start()
    table_arriving.start()
    for copy in arriving[1:]:
        copy.start()
    taps_arriving.wait()
    leaving = []
    for j in range(blocks):
        arriving[j].wait()
        start, length = (0, SB + extra) if j == 0 else (j * SB + extra, SB)
        for f in range(length):
            for n in range(0, FRAME, 128):
                frames[n // 128, 4 * (start + f) : 4 * (start + f) + 4, :] = x_held[
                    j, :, f * FRAME + n : f * FRAME + n + 128
                ].astype(jnp.float32)
        for n in range(0, FRAME, 128):
            taps = [taps_held[t : t + 1, n : n + 128] for t in range(TAPS)]
            for i in range(4):
                for s in range(j * SB, (j + 1) * SB, 16):
                    total = frames[n // 128, pl.ds(i + 4 * s, 16, stride=4), :] * taps[0]
                    for t in range(1, TAPS):
                        total = total + frames[n // 128, pl.ds(i + 4 * (s + t), 16, stride=4), :] * taps[t]
                    row = i * SB + s - j * SB
                    filtered[row : row + 16, n : n + 128] = total.astype(jnp.bfloat16)
        if j == 0:
            table_arriving.wait()
        for pair in range(2):
            product = lax.dot_general(
                table[...], filtered[pair * 2 * SB : (pair + 1) * 2 * SB, :], NT, preferred_element_type=jnp.float32
            )
            for p in range(2):
                part = product[p * CHAN : (p + 1) * CHAN]
                rows = jnp.concatenate(
                    [part[:, :SB].reshape(CHAN // 8, 8, SB), part[:, SB:].reshape(CHAN // 8, 8, SB)], axis=1
                )
                out_held[j, :, pair * 16 : pair * 16 + 16, p * SB : (p + 1) * SB] = rows.astype(jnp.bfloat16)
        if split:
            side = place_ref[2]
            sources = [out_held.at[j, pl.ds(side * 32, 32)], out_held.at[j, pl.ds((1 - side) * 32, 32)]]
        else:
            sources = [out_held.at[j]]
        for k, (source, out) in enumerate(zip(sources, outs)):
            copy = pltpu.make_async_copy(source, out.at[:, :, pl.ds(j * 2 * SB, 2 * SB)], out_sem.at[2 * j + k])
            copy.start()
            leaving.append(copy)
    for copy in leaving:
        copy.wait()


def filter_section(place, samples, pfb_taps, table, first, blocks, split):
    in_hbm = pl.BlockSpec(memory_space=pltpu.HBM)
    lanes = blocks * 2 * SB
    out_shape = [pltpu.HBM((32, 32, lanes), jnp.bfloat16)] * 2 if split else [pltpu.HBM((64, 32, lanes), jnp.bfloat16)]
    return pl.pallas_call(
        functools.partial(spectra_kernel, first, split),
        in_specs=[SMALL, in_hbm, in_hbm, in_hbm],
        out_specs=[in_hbm] * len(out_shape),
        out_shape=out_shape,
        scratch_shapes=[
            pltpu.VMEM((blocks, 4, (SB + TAPS - 1) * FRAME), jnp.bfloat16),
            pltpu.VMEM((2 * CHAN, FRAME), jnp.bfloat16),
            pltpu.VMEM((TAPS, FRAME), jnp.float32),
            pltpu.VMEM((FRAME // 128, 4 * (blocks * SB + 4), 128), jnp.float32),
            pltpu.VMEM((4 * SB, FRAME), jnp.bfloat16),
            pltpu.VMEM((blocks, 64, 32, 2 * SB), jnp.bfloat16),
            pltpu.SemaphoreType.DMA((blocks,)),
            pltpu.SemaphoreType.DMA,
            pltpu.SemaphoreType.DMA,
            pltpu.SemaphoreType.DMA((2 * blocks,)),
        ],
        compiler_params=pltpu.CompilerParams(vmem_limit_bytes=40 * 1024 * 1024),
        name="filter_section",
    )(place, *(pltpu.with_memory_space_constraint(a, pltpu.HBM) for a in (samples, table, pfb_taps)))


def merge_kernel(place_ref, stay_ref, got_ref, out_ref, held, sem):
    side = place_ref[2]
    held[:, side] = stay_ref[...]
    held[:, 1 - side] = got_ref[...]
    copy = pltpu.make_async_copy(held, out_ref, sem)
    copy.start()
    copy.wait()


def merge(place, stay, got):
    shape = (32, 2) + stay.shape[1:]
    return pl.pallas_call(
        merge_kernel,
        in_specs=[SMALL, IN_VMEM, IN_VMEM],
        out_specs=pl.BlockSpec(memory_space=pltpu.HBM),
        out_shape=pltpu.HBM(shape, jnp.bfloat16),
        scratch_shapes=[pltpu.VMEM(shape, jnp.bfloat16), pltpu.SemaphoreType.DMA],
        compiler_params=pltpu.CompilerParams(vmem_limit_bytes=40 * 1024 * 1024),
        name="merge_sides",
    )(place, stay, got)


def rows_kernel(place_ref, order_ref, source_ref, cross_ref, rest_ref, whole_ref, source, held, in_sem, out_sem, whole_sem):
    chip = place_ref[0]
    halves = (1 - chip, chip)
    arriving = []
    for k, half in enumerate(halves):
        part = source_ref.at[pl.ds(half * 32, 32)] if len(source_ref.shape) == 3 else source_ref.at[:, half]
        arriving.append(pltpu.make_async_copy(part, source.at[k], in_sem.at[k]))
        arriving[k].start()
    leaving = []
    for k, (half, out_ref) in enumerate(zip(halves, (cross_ref, rest_ref))):
        arriving[k].wait()
        for g in range(4):
            rows = source[k, g * 8 : (g + 1) * 8].reshape(256, source.shape[-1])
            turned = jnp.dot(order_ref[...], rows, preferred_element_type=jnp.float32).astype(jnp.bfloat16)
            for c in range(8):
                held[k, c, g * 32 : (g + 1) * 32, :] = turned[c * 32 : (c + 1) * 32]
        block_half = whole_ref.at[:, pl.ds(pl.multiple_of(half * 128, 128), 128)]
        leaving.append(pltpu.make_async_copy(held.at[k], out_ref, out_sem.at[k]))
        leaving.append(pltpu.make_async_copy(held.at[k], block_half, whole_sem.at[k]))
        leaving[-2].start()
        leaving[-1].start()
    for copy in leaving:
        copy.wait()


def channel_rows(place, order, source):
    lanes = source.shape[-1]
    in_hbm = pl.BlockSpec(memory_space=pltpu.HBM)
    shapes = [(8, 128, lanes), (8, 128, lanes), (8, BLOCK, lanes)]
    return pl.pallas_call(
        rows_kernel,
        in_specs=[SMALL, IN_VMEM, pl.BlockSpec(memory_space=pl.ANY)],
        out_specs=[in_hbm] * 3,
        out_shape=[pltpu.HBM(shape, jnp.bfloat16) for shape in shapes],
        scratch_shapes=[
            pltpu.VMEM((2, 32, 32, lanes), jnp.bfloat16),
            pltpu.VMEM((2, 8, 128, lanes), jnp.bfloat16),
            pltpu.SemaphoreType.DMA((2,)),
            pltpu.SemaphoreType.DMA((2,)),
            pltpu.SemaphoreType.DMA((2,)),
        ],
        compiler_params=pltpu.CompilerParams(vmem_limit_bytes=40 * 1024 * 1024),
        name="channel_rows",
    )(place, order, source)


def stacked(rows):
    pieces = []
    for s in range(0, rows.shape[1], 2 * SB):
        pieces += [rows[:, s + SB : s + 2 * SB], -rows[:, s : s + SB]]
    return jnp.concatenate([rows, jnp.concatenate(pieces, axis=1)], axis=0)


def tile_products(rows, cols):
    return lax.dot_general(stacked(rows), cols, NT, preferred_element_type=jnp.float32)


def self_kernel(own0_ref, own1_ref, self_ref, self_held, sem):
    copies = []
    for c in range(8):
        rows = jnp.concatenate([own0_ref[c], own1_ref[c]], axis=1)
        product = tile_products(rows, rows) * (1.0 / SPECTRA)
        self_held[0, c] = product[:BLOCK]
        self_held[1, c] = product[BLOCK:]
        copies.append(pltpu.make_async_copy(self_held.at[:, c], self_ref.at[:, c], sem.at[c]))
        copies[-1].start()
    for copy in copies:
        copy.wait()


def self_tiles(own0, own1):
    return pl.pallas_call(
        self_kernel,
        in_specs=[IN_VMEM] * 2,
        out_specs=pl.BlockSpec(memory_space=pltpu.HBM),
        out_shape=pltpu.HBM((2, 8, BLOCK, BLOCK), jnp.float32),
        scratch_shapes=[pltpu.VMEM((2, 8, BLOCK, BLOCK), jnp.float32), pltpu.SemaphoreType.DMA((8,))],
        compiler_params=pltpu.CompilerParams(vmem_limit_bytes=40 * 1024 * 1024),
        name="self_tiles",
    )(own0, own1)


def put_columns(place_ref, f_ref, g_ref, h_ref, s_ref, out_ref):
    chip = place_ref[0]

    @pl.when(place_ref[1] == 0)
    def _():
        out_ref[:, pl.ds(pl.multiple_of(chip * 128, 128), 128), :] = f_ref[...]
        out_ref[:, pl.ds(pl.multiple_of((1 - chip) * 128, 128), 128), :] = g_ref[...]

    @pl.when(place_ref[1] == 1)
    def _():
        out_ref[:, :BLOCK, :] = h_ref[...]

    out_ref[:, BLOCK:, :] = s_ref[...]


def early_kernel(place_ref, own_ref, f_ref, g_ref, h_ref, s_ref, out_ref, held):
    put_columns(place_ref, f_ref, g_ref, h_ref, s_ref, held)
    for c in range(8):
        out_ref[c] = tile_products(own_ref[c], held[c])


def early_products(place, own, *received):
    columns = BLOCK + BLOCK // 2
    return pl.pallas_call(
        early_kernel,
        in_specs=[SMALL] + [IN_VMEM] * 5,
        out_specs=IN_VMEM,
        out_shape=jax.ShapeDtypeStruct((8, 2 * BLOCK, columns), jnp.float32),
        scratch_shapes=[pltpu.VMEM((8, columns, own.shape[-1]), jnp.bfloat16)],
        compiler_params=pltpu.CompilerParams(vmem_limit_bytes=40 * 1024 * 1024),
        name="early_products",
    )(place, own, *received)


def cross_kernel(place_ref, own_ref, early_ref, f_ref, g_ref, h_ref, s_ref, prior_ref, far_ref,
                 held, prior_held, far_held, prior_sem, far_sem):
    put_columns(place_ref, f_ref, g_ref, h_ref, s_ref, held)
    copies = []
    for c in range(8):
        product = (tile_products(own_ref[c], held[c]) + early_ref[c]) * (1.0 / SPECTRA)
        for p in range(2):
            prior_held[p, c] = product[p * BLOCK : (p + 1) * BLOCK, :BLOCK]
            far_held[p, c] = product[p * BLOCK : (p + 1) * BLOCK, BLOCK:]
        copies.append(pltpu.make_async_copy(prior_held.at[:, c], prior_ref.at[:, c], prior_sem.at[c]))
        copies.append(pltpu.make_async_copy(far_held.at[:, c], far_ref.at[:, c], far_sem.at[c]))
        copies[-2].start()
        copies[-1].start()
    for copy in copies:
        copy.wait()


def cross_tiles(place, own, early, *late):
    in_hbm = pl.BlockSpec(memory_space=pltpu.HBM)
    prior_shape, far_shape = (2, 8, BLOCK, BLOCK), (2, 8, BLOCK, BLOCK // 2)
    return pl.pallas_call(
        cross_kernel,
        in_specs=[SMALL] + [IN_VMEM] * (2 + len(late)),
        out_specs=[in_hbm, in_hbm],
        out_shape=[pltpu.HBM(prior_shape, jnp.float32), pltpu.HBM(far_shape, jnp.float32)],
        scratch_shapes=[
            pltpu.VMEM((8, BLOCK + BLOCK // 2, late[0].shape[-1]), jnp.bfloat16),
            pltpu.VMEM(prior_shape, jnp.float32),
            pltpu.VMEM(far_shape, jnp.float32),
            pltpu.SemaphoreType.DMA((8,)),
            pltpu.SemaphoreType.DMA((8,)),
        ],
        compiler_params=pltpu.CompilerParams(vmem_limit_bytes=40 * 1024 * 1024),
        name="cross_tiles",
    )(place, own, early, *late)


CROSSED = [(0, 3), (1, 2), (2, 1), (3, 0)]
ODD_OVER = [(1, 2), (3, 0)]
EVEN_UP = [(0, 1), (2, 3)]
SWAPPED = [(0, 1), (1, 0), (2, 3), (3, 2)]


def on_device(table, order, samples, pfb_taps):
    position = lax.axis_index("narrow")
    place = jnp.stack([position // 2, position % 2, lax.axis_index("side")]).astype(jnp.int32)

    def exchange(crossing, rest, whole):
        f = lax.ppermute(crossing, "narrow", CROSSED)
        g = lax.ppermute(rest, "narrow", ODD_OVER)
        h = lax.ppermute(whole, "narrow", EVEN_UP)
        return f, g, h

    def swap(f):
        return lax.ppermute(f, "narrow", SWAPPED)

    (early,) = filter_section(place, samples, pfb_taps, table, 0, EARLY, False)
    stay, leave = filter_section(place, samples, pfb_taps, table, EARLY * SB, 1, True)
    source0 = lax.all_to_all(early, ("side", "plane"), split_axis=0, concat_axis=0, tiled=True)
    late = merge(place, stay, lax.ppermute(leave, "side", [(0, 1), (1, 0)]))
    late, source0 = lax.optimization_barrier((late, source0))
    source1 = lax.all_to_all(late, "plane", split_axis=0, concat_axis=0, tiled=True)
    crossing0, rest0, own0 = channel_rows(place, order, source0)
    f0, g0, h0 = exchange(crossing0, rest0, own0)
    s0 = swap(f0)
    source1, f0, g0, h0, s0 = lax.optimization_barrier((source1, f0, g0, h0, s0))
    crossing1, rest1, own1 = channel_rows(place, order, source1)
    f1, g1, h1 = exchange(crossing1, rest1, own1)
    own0, own1, f0, h1 = lax.optimization_barrier((own0, own1, f0, h1))
    early = early_products(place, own0, f0, g0, h0, s0)
    self_vis = self_tiles(own0, own1)
    f1, self_vis, early = lax.optimization_barrier((f1, self_vis, early))
    prior_vis, far_vis = cross_tiles(place, own1, early, f1, g1, h1, swap(f1))
    return (self_vis, prior_vis, far_vis)


def solution(mesh):
    parted = Mesh(mesh.devices.reshape(2, mesh.devices.shape[0] // 2, mesh.devices.shape[1]), ("side", "plane", "narrow"))
    out_spec = P(None, ("side", "plane"), "narrow", None)
    return jax.shard_map(
        functools.partial(on_device, dft_table(), row_order()),
        mesh=parted,
        in_specs=(P(("narrow", "side", "plane"), None), P()),
        out_specs=(out_spec, out_spec, out_spec),
        check_vma=False,
    )
```

```python
import functools
import math

import jax
import jax.numpy as jnp
import numpy as np
from jax import lax
from jax.experimental import pallas as pl
from jax.experimental.pallas import tpu as pltpu
from jax.sharding import Mesh
from jax.sharding import PartitionSpec as P

CHAN = 512
TAPS = 4
SPECTRA = 384
BLOCK = 256
FRAME = 2 * CHAN
SB = 128
EARLY = 2
NT = (((1,), (1,)), ((), ()))
SMALL = pl.BlockSpec(memory_space=pltpu.SMEM)
IN_VMEM = pl.BlockSpec(memory_space=pltpu.VMEM)


def dft_table():
    positions = np.arange(FRAME, dtype=np.int32)
    bins = np.arange(CHAN, dtype=np.int32)
    phases = bins[:, None] * positions[None, :] % FRAME
    angles = phases.astype(np.float32) * np.float32(math.pi / CHAN)
    norming = np.float32(FRAME ** (-0.5))
    table = np.concatenate([np.cos(angles) * norming, -np.sin(angles) * norming])
    return table.astype(jnp.bfloat16)


def row_order():
    order = np.arange(256).reshape(32, 8).T.reshape(-1)
    return np.eye(256, dtype=np.float32)[order].astype(jnp.bfloat16)


def spectra_kernel(first, split, place_ref, x_ref, table_ref, taps_ref, *refs):
    outs, (x_held, table, taps_held, frames, filtered, out_held, x_sem, table_sem, taps_sem, out_sem) = refs[:-10], refs[-10:]
    blocks = x_held.shape[0]
    extra = TAPS - 1
    arriving = []
    for j in range(blocks):
        start, length = (first, SB + extra) if j == 0 else (first + j * SB + extra, SB)
        arriving.append(
            pltpu.make_async_copy(
                x_ref.at[:, pl.ds(start * FRAME, length * FRAME)], x_held.at[j, :, pl.ds(0, length * FRAME)], x_sem.at[j]
            )
        )
    table_arriving = pltpu.make_async_copy(table_ref, table, table_sem)
    taps_arriving = pltpu.make_async_copy(taps_ref, taps_held, taps_sem)
    taps_arriving.start()
    arriving[0].start()
    table_arriving.start()
    for copy in arriving[1:]:
        copy.start()
    taps_arriving.wait()
    leaving = []
    for j in range(blocks):
        arriving[j].wait()
        start, length = (0, SB + extra) if j == 0 else (j * SB + extra, SB)
        for f in range(length):
            for n in range(0, FRAME, 128):
                frames[n // 128, 4 * (start + f) : 4 * (start + f) + 4, :] = x_held[
                    j, :, f * FRAME + n : f * FRAME + n + 128
                ].astype(jnp.float32)
        for n in range(0, FRAME, 128):
            taps = [taps_held[t : t + 1, n : n + 128] for t in range(TAPS)]
            for i in range(4):
                for s in range(j * SB, (j + 1) * SB, 16):
                    total = frames[n // 128, pl.ds(i + 4 * s, 16, stride=4), :] * taps[0]
                    for t in range(1, TAPS):
                        total = total + frames[n // 128, pl.ds(i + 4 * (s + t), 16, stride=4), :] * taps[t]
                    row = i * SB + s - j * SB
                    filtered[row : row + 16, n : n + 128] = total.astype(jnp.bfloat16)
        if j == 0:
            table_arriving.wait()
        for pair in range(2):
            product = lax.dot_general(
                table[...], filtered[pair * 2 * SB : (pair + 1) * 2 * SB, :], NT, preferred_element_type=jnp.float32
            )
            for p in range(2):
                part = product[p * CHAN : (p + 1) * CHAN]
                rows = jnp.concatenate(
                    [part[:, :SB].reshape(CHAN // 8, 8, SB), part[:, SB:].reshape(CHAN // 8, 8, SB)], axis=1
                )
                out_held[j, :, pair * 16 : pair * 16 + 16, p * SB : (p + 1) * SB] = rows.astype(jnp.bfloat16)
        if split:
            side = place_ref[2]
            sources = [out_held.at[j, pl.ds(side * 32, 32)], out_held.at[j, pl.ds((1 - side) * 32, 32)]]
        else:
            sources = [out_held.at[j]]
        for k, (source, out) in enumerate(zip(sources, outs)):
            copy = pltpu.make_async_copy(source, out.at[:, :, pl.ds(j * 2 * SB, 2 * SB)], out_sem.at[2 * j + k])
            copy.start()
            leaving.append(copy)
    for copy in leaving:
        copy.wait()


def filter_section(place, samples, pfb_taps, table, first, blocks, split):
    in_hbm = pl.BlockSpec(memory_space=pltpu.HBM)
    lanes = blocks * 2 * SB
    out_shape = [pltpu.HBM((32, 32, lanes), jnp.bfloat16)] * 2 if split else [pltpu.HBM((64, 32, lanes), jnp.bfloat16)]
    return pl.pallas_call(
        functools.partial(spectra_kernel, first, split),
        in_specs=[SMALL, in_hbm, in_hbm, in_hbm],
        out_specs=[in_hbm] * len(out_shape),
        out_shape=out_shape,
        scratch_shapes=[
            pltpu.VMEM((blocks, 4, (SB + TAPS - 1) * FRAME), jnp.bfloat16),
            pltpu.VMEM((2 * CHAN, FRAME), jnp.bfloat16),
            pltpu.VMEM((TAPS, FRAME), jnp.float32),
            pltpu.VMEM((FRAME // 128, 4 * (blocks * SB + 4), 128), jnp.float32),
            pltpu.VMEM((4 * SB, FRAME), jnp.bfloat16),
            pltpu.VMEM((blocks, 64, 32, 2 * SB), jnp.bfloat16),
            pltpu.SemaphoreType.DMA((blocks,)),
            pltpu.SemaphoreType.DMA,
            pltpu.SemaphoreType.DMA,
            pltpu.SemaphoreType.DMA((2 * blocks,)),
        ],
        compiler_params=pltpu.CompilerParams(vmem_limit_bytes=40 * 1024 * 1024),
        name="filter_section",
    )(place, *(pltpu.with_memory_space_constraint(a, pltpu.HBM) for a in (samples, table, pfb_taps)))


def merge_kernel(place_ref, stay_ref, got_ref, far_ref, out_ref, held, sem):
    side = place_ref[2]
    held[:, side] = stay_ref[...]
    held[:, 1 - side] = got_ref[...]
    held[:, 2] = far_ref[...]
    copy = pltpu.make_async_copy(held, out_ref, sem)
    copy.start()
    copy.wait()


def merge(place, stay, got, far):
    shape = (32, 3) + stay.shape[1:]
    return pl.pallas_call(
        merge_kernel,
        in_specs=[SMALL] + [IN_VMEM] * 3,
        out_specs=pl.BlockSpec(memory_space=pltpu.HBM),
        out_shape=pltpu.HBM(shape, jnp.bfloat16),
        scratch_shapes=[pltpu.VMEM(shape, jnp.bfloat16), pltpu.SemaphoreType.DMA],
        compiler_params=pltpu.CompilerParams(vmem_limit_bytes=40 * 1024 * 1024),
        name="merge_sides",
    )(place, stay, got, far)


def rows_kernel(place_ref, order_ref, source_ref, first_ref, second_ref, whole_ref, source, held, in_sem, out_sem, whole_sem):
    chip = place_ref[0]
    late = len(source_ref.shape) == 4
    if late:
        parts = [source_ref.at[:, chip], source_ref.at[:, 2], source_ref.at[:, 1 - chip]]
        steps = [(first_ref, chip), (second_ref, None), (None, 1 - chip)]
    else:
        parts = [source_ref.at[pl.ds(half * 32, 32)] for half in (1 - chip, chip)]
        steps = [(first_ref, 1 - chip), (second_ref, chip)]
    arriving = [pltpu.make_async_copy(part, source.at[k], in_sem.at[k]) for k, part in enumerate(parts)]
    for copy in arriving:
        copy.start()
    leaving = []
    for k, (out_ref, half) in enumerate(steps):
        arriving[k].wait()
        for g in range(4):
            rows = source[k, g * 8 : (g + 1) * 8].reshape(256, source.shape[-1])
            turned = jnp.dot(order_ref[...], rows, preferred_element_type=jnp.float32).astype(jnp.bfloat16)
            for c in range(8):
                held[k, c, g * 32 : (g + 1) * 32, :] = turned[c * 32 : (c + 1) * 32]
        if out_ref is not None:
            leaving.append(pltpu.make_async_copy(held.at[k], out_ref, out_sem.at[k]))
            leaving[-1].start()
        if half is not None:
            block_half = whole_ref.at[:, pl.ds(pl.multiple_of(half * 128, 128), 128)]
            leaving.append(pltpu.make_async_copy(held.at[k], block_half, whole_sem.at[k]))
            leaving[-1].start()
    for copy in leaving:
        copy.wait()


def channel_rows(place, order, source):
    lanes = source.shape[-1]
    count = 3 if source.ndim == 4 else 2
    in_hbm = pl.BlockSpec(memory_space=pltpu.HBM)
    shapes = [(8, 128, lanes), (8, 128, lanes), (8, BLOCK, lanes)]
    return pl.pallas_call(
        rows_kernel,
        in_specs=[SMALL, IN_VMEM, pl.BlockSpec(memory_space=pl.ANY)],
        out_specs=[in_hbm] * 3,
        out_shape=[pltpu.HBM(shape, jnp.bfloat16) for shape in shapes],
        scratch_shapes=[
            pltpu.VMEM((count, 32, 32, lanes), jnp.bfloat16),
            pltpu.VMEM((count, 8, 128, lanes), jnp.bfloat16),
            pltpu.SemaphoreType.DMA((count,)),
            pltpu.SemaphoreType.DMA((count,)),
            pltpu.SemaphoreType.DMA((count,)),
        ],
        compiler_params=pltpu.CompilerParams(vmem_limit_bytes=40 * 1024 * 1024),
        name="channel_rows",
    )(place, order, source)


def stacked(rows):
    pieces = []
    for s in range(0, rows.shape[1], 2 * SB):
        pieces += [rows[:, s + SB : s + 2 * SB], -rows[:, s : s + SB]]
    return jnp.concatenate([rows, jnp.concatenate(pieces, axis=1)], axis=0)


def tile_products(rows, cols):
    return lax.dot_general(stacked(rows), cols, NT, preferred_element_type=jnp.float32)


def self_kernel(own0_ref, own1_ref, self_ref, self_held, sem):
    copies = []
    for c in range(8):
        rows = jnp.concatenate([own0_ref[c], own1_ref[c]], axis=1)
        product = tile_products(rows, rows) * (1.0 / SPECTRA)
        self_held[0, c] = product[:BLOCK]
        self_held[1, c] = product[BLOCK:]
        copies.append(pltpu.make_async_copy(self_held.at[:, c], self_ref.at[:, c], sem.at[c]))
        copies[-1].start()
    for copy in copies:
        copy.wait()


def self_tiles(own0, own1):
    return pl.pallas_call(
        self_kernel,
        in_specs=[IN_VMEM] * 2,
        out_specs=pl.BlockSpec(memory_space=pltpu.HBM),
        out_shape=pltpu.HBM((2, 8, BLOCK, BLOCK), jnp.float32),
        scratch_shapes=[pltpu.VMEM((2, 8, BLOCK, BLOCK), jnp.float32), pltpu.SemaphoreType.DMA((8,))],
        compiler_params=pltpu.CompilerParams(vmem_limit_bytes=40 * 1024 * 1024),
        name="self_tiles",
    )(own0, own1)


def put_columns(place_ref, f_ref, g_ref, h_ref, s_ref, out_ref):
    chip = place_ref[0]

    @pl.when(place_ref[1] == 0)
    def _():
        out_ref[:, pl.ds(pl.multiple_of(chip * 128, 128), 128), :] = f_ref[...]
        out_ref[:, pl.ds(pl.multiple_of((1 - chip) * 128, 128), 128), :] = g_ref[...]

    @pl.when(place_ref[1] == 1)
    def _():
        out_ref[:, :BLOCK, :] = h_ref[...]

    out_ref[:, BLOCK:, :] = s_ref[...]


def early_kernel(place_ref, f_ref, g_ref, h_ref, s_ref, out_ref):
    put_columns(place_ref, f_ref, g_ref, h_ref, s_ref, out_ref)


def early_columns(place, *received):
    return pl.pallas_call(
        early_kernel,
        in_specs=[SMALL] + [IN_VMEM] * 4,
        out_specs=IN_VMEM,
        out_shape=jax.ShapeDtypeStruct((8, BLOCK + BLOCK // 2, received[0].shape[-1]), jnp.bfloat16),
        compiler_params=pltpu.CompilerParams(vmem_limit_bytes=40 * 1024 * 1024),
        name="early_columns",
    )(place, *received)


def cross_kernel(place_ref, own0_ref, own1_ref, early_ref, f_ref, g_ref, h_ref, s_ref, prior_ref, far_ref,
                 held, prior_held, far_held, prior_sem, far_sem):
    put_columns(place_ref, f_ref, g_ref, h_ref, s_ref, held)
    copies = []
    for c in range(8):
        rows = jnp.concatenate([own0_ref[c], own1_ref[c]], axis=1)
        product = tile_products(rows, jnp.concatenate([early_ref[c], held[c]], axis=1)) * (1.0 / SPECTRA)
        for p in range(2):
            prior_held[p, c] = product[p * BLOCK : (p + 1) * BLOCK, :BLOCK]
            far_held[p, c] = product[p * BLOCK : (p + 1) * BLOCK, BLOCK:]
        copies.append(pltpu.make_async_copy(prior_held.at[:, c], prior_ref.at[:, c], prior_sem.at[c]))
        copies.append(pltpu.make_async_copy(far_held.at[:, c], far_ref.at[:, c], far_sem.at[c]))
        copies[-2].start()
        copies[-1].start()
    for copy in copies:
        copy.wait()


def cross_tiles(place, own0, own1, early, *late):
    in_hbm = pl.BlockSpec(memory_space=pltpu.HBM)
    prior_shape, far_shape = (2, 8, BLOCK, BLOCK), (2, 8, BLOCK, BLOCK // 2)
    return pl.pallas_call(
        cross_kernel,
        in_specs=[SMALL] + [IN_VMEM] * (3 + len(late)),
        out_specs=[in_hbm, in_hbm],
        out_shape=[pltpu.HBM(prior_shape, jnp.float32), pltpu.HBM(far_shape, jnp.float32)],
        scratch_shapes=[
            pltpu.VMEM((8, BLOCK + BLOCK // 2, late[0].shape[-1]), jnp.bfloat16),
            pltpu.VMEM(prior_shape, jnp.float32),
            pltpu.VMEM(far_shape, jnp.float32),
            pltpu.SemaphoreType.DMA((8,)),
            pltpu.SemaphoreType.DMA((8,)),
        ],
        compiler_params=pltpu.CompilerParams(vmem_limit_bytes=40 * 1024 * 1024),
        name="cross_tiles",
    )(place, own0, own1, early, *late)


CROSSED = [(0, 3), (1, 2), (2, 1), (3, 0)]
ODD_OVER = [(1, 2), (3, 0)]
EVEN_UP = [(0, 1), (2, 3)]
SWAPPED = [(0, 1), (1, 0), (2, 3), (3, 2)]


def on_device(table, order, samples, pfb_taps):
    position = lax.axis_index("narrow")
    place = jnp.stack([position // 2, position % 2, lax.axis_index("side")]).astype(jnp.int32)

    def exchange(crossing, rest, whole):
        f = lax.ppermute(crossing, "narrow", CROSSED)
        g = lax.ppermute(rest, "narrow", ODD_OVER)
        h = lax.ppermute(whole, "narrow", EVEN_UP)
        return f, g, h

    def swap(f):
        return lax.ppermute(f, "narrow", SWAPPED)

    (early,) = filter_section(place, samples, pfb_taps, table, 0, EARLY, False)
    stay, leave = filter_section(place, samples, pfb_taps, table, EARLY * SB, 1, True)
    source0 = lax.all_to_all(early, ("side", "plane"), split_axis=0, concat_axis=0, tiled=True)
    got = lax.ppermute(leave, "side", [(0, 1), (1, 0)])
    far = lax.ppermute(jnp.where(place[2] == 1 - place[0], stay, got), "narrow", CROSSED)
    late = merge(place, stay, got, far)
    late, source0 = lax.optimization_barrier((late, source0))
    source1 = lax.all_to_all(late, "plane", split_axis=0, concat_axis=0, tiled=True)
    crossing0, rest0, own0 = channel_rows(place, order, source0)
    f0, g0, h0 = exchange(crossing0, rest0, own0)
    s0 = swap(f0)
    source1, f0 = lax.optimization_barrier((source1, f0))
    rest1, f1, own1 = channel_rows(place, order, source1)
    g1 = lax.ppermute(rest1, "narrow", ODD_OVER)
    h1 = lax.ppermute(own1, "narrow", EVEN_UP)
    s1 = swap(f1)
    own0, own1, h1 = lax.optimization_barrier((own0, own1, h1))
    self_vis = self_tiles(own0, own1)
    held0 = early_columns(place, f0, g0, h0, s0)
    g1, self_vis, held0 = lax.optimization_barrier((g1, self_vis, held0))
    prior_vis, far_vis = cross_tiles(place, own0, own1, held0, f1, g1, h1, s1)
    return (self_vis, prior_vis, far_vis)


def solution(mesh):
    parted = Mesh(mesh.devices.reshape(2, mesh.devices.shape[0] // 2, mesh.devices.shape[1]), ("side", "plane", "narrow"))
    out_spec = P(None, ("side", "plane"), "narrow", None)
    return jax.shard_map(
        functools.partial(on_device, dft_table(), row_order()),
        mesh=parted,
        in_specs=(P(("narrow", "side", "plane"), None), P()),
        out_specs=(out_spec, out_spec, out_spec),
        check_vma=False,
    )
```

```python
import functools
import math

import jax
import jax.numpy as jnp
import numpy as np
from jax import lax
from jax.experimental import pallas as pl
from jax.experimental.pallas import tpu as pltpu
from jax.sharding import Mesh
from jax.sharding import PartitionSpec as P

CHAN = 512
TAPS = 4
SPECTRA = 384
BLOCK = 256
FRAME = 2 * CHAN
SB = 128
EARLY = 2
NT = (((1,), (1,)), ((), ()))
SMALL = pl.BlockSpec(memory_space=pltpu.SMEM)
IN_VMEM = pl.BlockSpec(memory_space=pltpu.VMEM)


def dft_table():
    positions = np.arange(FRAME, dtype=np.int32)
    bins = np.arange(CHAN, dtype=np.int32)
    phases = bins[:, None] * positions[None, :] % FRAME
    angles = phases.astype(np.float32) * np.float32(math.pi / CHAN)
    norming = np.float32(FRAME ** (-0.5))
    table = np.concatenate([np.cos(angles) * norming, -np.sin(angles) * norming])
    return table.astype(jnp.bfloat16)


def row_order():
    order = np.arange(256).reshape(32, 8).T.reshape(-1)
    return np.eye(256, dtype=np.float32)[order].astype(jnp.bfloat16)


def spectra_kernel(first, split, place_ref, x_ref, table_ref, taps_ref, *refs):
    outs, (x_held, table, taps_held, frames, filtered, out_held, x_sem, table_sem, taps_sem, out_sem) = refs[:-10], refs[-10:]
    blocks = x_held.shape[0]
    extra = TAPS - 1
    arriving = []
    for j in range(blocks):
        start, length = (first, SB + extra) if j == 0 else (first + j * SB + extra, SB)
        arriving.append(
            pltpu.make_async_copy(
                x_ref.at[:, pl.ds(start * FRAME, length * FRAME)], x_held.at[j, :, pl.ds(0, length * FRAME)], x_sem.at[j]
            )
        )
    table_arriving = pltpu.make_async_copy(table_ref, table, table_sem)
    taps_arriving = pltpu.make_async_copy(taps_ref, taps_held, taps_sem)
    taps_arriving.start()
    arriving[0].start()
    table_arriving.start()
    for copy in arriving[1:]:
        copy.start()
    taps_arriving.wait()
    leaving = []
    for j in range(blocks):
        arriving[j].wait()
        start, length = (0, SB + extra) if j == 0 else (j * SB + extra, SB)
        for f in range(length):
            for n in range(0, FRAME, 128):
                frames[n // 128, 4 * (start + f) : 4 * (start + f) + 4, :] = x_held[
                    j, :, f * FRAME + n : f * FRAME + n + 128
                ].astype(jnp.float32)
        for n in range(0, FRAME, 128):
            taps = [taps_held[t : t + 1, n : n + 128] for t in range(TAPS)]
            for i in range(4):
                for s in range(j * SB, (j + 1) * SB, 16):
                    total = frames[n // 128, pl.ds(i + 4 * s, 16, stride=4), :] * taps[0]
                    for t in range(1, TAPS):
                        total = total + frames[n // 128, pl.ds(i + 4 * (s + t), 16, stride=4), :] * taps[t]
                    row = i * SB + s - j * SB
                    filtered[row : row + 16, n : n + 128] = total.astype(jnp.bfloat16)
        if j == 0:
            table_arriving.wait()
        for pair in range(2):
            product = lax.dot_general(
                table[...], filtered[pair * 2 * SB : (pair + 1) * 2 * SB, :], NT, preferred_element_type=jnp.float32
            )
            for p in range(2):
                part = product[p * CHAN : (p + 1) * CHAN]
                rows = jnp.concatenate(
                    [part[:, :SB].reshape(CHAN // 8, 8, SB), part[:, SB:].reshape(CHAN // 8, 8, SB)], axis=1
                )
                out_held[j, :, pair * 16 : pair * 16 + 16, p * SB : (p + 1) * SB] = rows.astype(jnp.bfloat16)
        if split:
            side = place_ref[2]
            sources = [out_held.at[j, pl.ds(side * 32, 32)], out_held.at[j, pl.ds((1 - side) * 32, 32)]]
        else:
            sources = [out_held.at[j]]
        for k, (source, out) in enumerate(zip(sources, outs)):
            copy = pltpu.make_async_copy(source, out.at[:, :, pl.ds(j * 2 * SB, 2 * SB)], out_sem.at[2 * j + k])
            copy.start()
            leaving.append(copy)
    for copy in leaving:
        copy.wait()


def filter_section(place, samples, pfb_taps, table, first, blocks, split):
    in_hbm = pl.BlockSpec(memory_space=pltpu.HBM)
    lanes = blocks * 2 * SB
    out_shape = [pltpu.HBM((32, 32, lanes), jnp.bfloat16)] * 2 if split else [pltpu.HBM((64, 32, lanes), jnp.bfloat16)]
    return pl.pallas_call(
        functools.partial(spectra_kernel, first, split),
        in_specs=[SMALL, in_hbm, in_hbm, in_hbm],
        out_specs=[in_hbm] * len(out_shape),
        out_shape=out_shape,
        scratch_shapes=[
            pltpu.VMEM((blocks, 4, (SB + TAPS - 1) * FRAME), jnp.bfloat16),
            pltpu.VMEM((2 * CHAN, FRAME), jnp.bfloat16),
            pltpu.VMEM((TAPS, FRAME), jnp.float32),
            pltpu.VMEM((FRAME // 128, 4 * (blocks * SB + 4), 128), jnp.float32),
            pltpu.VMEM((4 * SB, FRAME), jnp.bfloat16),
            pltpu.VMEM((blocks, 64, 32, 2 * SB), jnp.bfloat16),
            pltpu.SemaphoreType.DMA((blocks,)),
            pltpu.SemaphoreType.DMA,
            pltpu.SemaphoreType.DMA,
            pltpu.SemaphoreType.DMA((2 * blocks,)),
        ],
        compiler_params=pltpu.CompilerParams(vmem_limit_bytes=20 * 1024 * 1024),
        name="filter_section",
    )(place, *(pltpu.with_memory_space_constraint(a, pltpu.HBM) for a in (samples, table, pfb_taps)))


def merge_kernel(place_ref, stay_ref, got_ref, over_ref, across_ref, out_ref, held, sem):
    side = place_ref[2]
    held[:, side] = stay_ref[...]
    held[:, 1 - side] = got_ref[...]

    @pl.when(side == place_ref[0])
    def _():
        held[:, 2] = over_ref[...]

    @pl.when(side != place_ref[0])
    def _():
        held[:, 2] = across_ref[...]

    copy = pltpu.make_async_copy(held, out_ref, sem)
    copy.start()
    copy.wait()


def merge(place, stay, got, over, across):
    shape = (32, 3) + stay.shape[1:]
    return pl.pallas_call(
        merge_kernel,
        in_specs=[SMALL] + [IN_VMEM] * 4,
        out_specs=pl.BlockSpec(memory_space=pltpu.HBM),
        out_shape=pltpu.HBM(shape, jnp.bfloat16),
        scratch_shapes=[pltpu.VMEM(shape, jnp.bfloat16), pltpu.SemaphoreType.DMA],
        compiler_params=pltpu.CompilerParams(vmem_limit_bytes=8 * 1024 * 1024),
        name="merge_sides",
    )(place, stay, got, over, across)


def order_rows(order_ref, source, held):
    for g in range(4):
        rows = source[g * 8 : (g + 1) * 8].reshape(256, source.shape[-1])
        turned = jnp.dot(order_ref[...], rows, preferred_element_type=jnp.float32).astype(jnp.bfloat16)
        for c in range(8):
            held[c, g * 32 : (g + 1) * 32, :] = turned[c * 32 : (c + 1) * 32]


def early_rows_kernel(place_ref, order_ref, source_ref, cross_ref, rest_ref, whole_ref, source, held, in_sem, out_sem, whole_sem):
    chip = place_ref[0]
    halves = (1 - chip, chip)
    arriving = [
        pltpu.make_async_copy(source_ref.at[pl.ds(half * 32, 32)], source.at[k], in_sem.at[k]) for k, half in enumerate(halves)
    ]
    for copy in arriving:
        copy.start()
    leaving = []
    for k, (half, out_ref) in enumerate(zip(halves, (cross_ref, rest_ref))):
        arriving[k].wait()
        order_rows(order_ref, source.at[k], held.at[k])
        block_half = whole_ref.at[:, pl.ds(pl.multiple_of(half * 128, 128), 128)]
        leaving.append(pltpu.make_async_copy(held.at[k], out_ref, out_sem.at[k]))
        leaving.append(pltpu.make_async_copy(held.at[k], block_half, whole_sem.at[k]))
        leaving[-2].start()
        leaving[-1].start()
    for copy in leaving:
        copy.wait()


def rows_call(kernel, count, place, order, source, shapes, name):
    lanes = source.shape[-1]
    in_hbm = pl.BlockSpec(memory_space=pltpu.HBM)
    return pl.pallas_call(
        kernel,
        in_specs=[SMALL, IN_VMEM, pl.BlockSpec(memory_space=pl.ANY)],
        out_specs=[in_hbm] * len(shapes),
        out_shape=[pltpu.HBM(shape, jnp.bfloat16) for shape in shapes],
        scratch_shapes=[
            pltpu.VMEM((count, 32, 32, lanes), jnp.bfloat16),
            pltpu.VMEM((count, 8, 128, lanes), jnp.bfloat16),
            pltpu.SemaphoreType.DMA((count,)),
            pltpu.SemaphoreType.DMA((count,)),
        ] + ([pltpu.SemaphoreType.DMA((count,))] if len(shapes) > count else []),
        compiler_params=pltpu.CompilerParams(vmem_limit_bytes=12 * 1024 * 1024),
        name=name,
    )(place, order, source)


def early_rows(place, order, source):
    lanes = source.shape[-1]
    shapes = [(8, 128, lanes), (8, 128, lanes), (8, BLOCK, lanes)]
    return rows_call(early_rows_kernel, 2, place, order, source, shapes, "early_rows")


def late_rows_kernel(rest, place_ref, order_ref, source_ref, *refs):
    outs, (source, held, in_sem, out_sem) = refs[:-4], refs[-4:]
    chip = place_ref[0]
    slots = (chip,) if rest else (1 - chip, 2)
    arriving = [pltpu.make_async_copy(source_ref.at[:, slot], source.at[k], in_sem.at[k]) for k, slot in enumerate(slots)]
    for copy in arriving:
        copy.start()
    leaving = []
    for k, out_ref in enumerate(outs):
        arriving[k].wait()
        order_rows(order_ref, source.at[k], held.at[k])
        leaving.append(pltpu.make_async_copy(held.at[k], out_ref, out_sem.at[k]))
        leaving[-1].start()
    for copy in leaving:
        copy.wait()


def late_rows(place, order, source, rest):
    count = 1 if rest else 2
    shapes = [(8, 128, source.shape[-1])] * count
    return rows_call(functools.partial(late_rows_kernel, rest), count, place, order, source, shapes, "late_rows")


def stacked(rows):
    pieces = []
    for s in range(0, rows.shape[1], 2 * SB):
        pieces += [rows[:, s + SB : s + 2 * SB], -rows[:, s : s + SB]]
    return jnp.concatenate([rows, jnp.concatenate(pieces, axis=1)], axis=0)


def tile_products(rows, cols):
    return lax.dot_general(stacked(rows), cols, NT, preferred_element_type=jnp.float32)


def put_halves(place_ref, chips_ref, others_ref, out_ref):
    chip = place_ref[0]
    out_ref[:, pl.ds(pl.multiple_of(chip * 128, 128), 128), :] = chips_ref[...]
    out_ref[:, pl.ds(pl.multiple_of((1 - chip) * 128, 128), 128), :] = others_ref[...]


def self_kernel(place_ref, own0_ref, crossing1_ref, rest1_ref, self_ref, own1, self_held, sem):
    put_halves(place_ref, rest1_ref, crossing1_ref, own1)
    copies = []
    for c in range(8):
        rows = jnp.concatenate([own0_ref[c], own1[c]], axis=1)
        product = tile_products(rows, rows) * (1.0 / SPECTRA)
        self_held[0, c] = product[:BLOCK]
        self_held[1, c] = product[BLOCK:]
        copies.append(pltpu.make_async_copy(self_held.at[:, c], self_ref.at[:, c], sem.at[c]))
        copies[-1].start()
    for copy in copies:
        copy.wait()


def self_tiles(place, *own):
    return pl.pallas_call(
        self_kernel,
        in_specs=[SMALL] + [IN_VMEM] * 3,
        out_specs=pl.BlockSpec(memory_space=pltpu.HBM),
        out_shape=pltpu.HBM((2, 8, BLOCK, BLOCK), jnp.float32),
        scratch_shapes=[
            pltpu.VMEM((8, BLOCK, own[1].shape[-1]), jnp.bfloat16),
            pltpu.VMEM((2, 8, BLOCK, BLOCK), jnp.float32),
            pltpu.SemaphoreType.DMA((8,)),
        ],
        compiler_params=pltpu.CompilerParams(vmem_limit_bytes=14 * 1024 * 1024),
        name="self_tiles",
    )(place, *own)


def early_kernel(place_ref, f_ref, g_ref, h_ref, s_ref, out_ref):
    @pl.when(place_ref[1] == 0)
    def _():
        put_halves(place_ref, f_ref, g_ref, out_ref)

    @pl.when(place_ref[1] == 1)
    def _():
        out_ref[:, :BLOCK, :] = h_ref[...]

    out_ref[:, BLOCK:, :] = s_ref[...]


def early_columns(place, *received):
    return pl.pallas_call(
        early_kernel,
        in_specs=[SMALL] + [IN_VMEM] * 4,
        out_specs=IN_VMEM,
        out_shape=jax.ShapeDtypeStruct((8, BLOCK + BLOCK // 2, received[0].shape[-1]), jnp.bfloat16),
        compiler_params=pltpu.CompilerParams(vmem_limit_bytes=8 * 1024 * 1024),
        name="early_columns",
    )(place, *received)


def cross_kernel(place_ref, own0_ref, early_ref, crossing_ref, rest_ref, f_ref, r_ref, h_ref, s_ref, prior_ref, far_ref,
                 own1, held, prior_held, far_held, prior_sem, far_sem):
    put_halves(place_ref, rest_ref, crossing_ref, own1)

    @pl.when(place_ref[1] == 0)
    def _():
        put_halves(place_ref, f_ref, r_ref, held)

    @pl.when(place_ref[1] == 1)
    def _():
        put_halves(place_ref, r_ref, h_ref, held)

    held[:, BLOCK:, :] = s_ref[...]
    copies = []
    for c in range(8):
        rows = jnp.concatenate([own0_ref[c], own1[c]], axis=1)
        product = tile_products(rows, jnp.concatenate([early_ref[c], held[c]], axis=1)) * (1.0 / SPECTRA)
        for p in range(2):
            prior_held[p, c] = product[p * BLOCK : (p + 1) * BLOCK, :BLOCK]
            far_held[p, c] = product[p * BLOCK : (p + 1) * BLOCK, BLOCK:]
        copies.append(pltpu.make_async_copy(prior_held.at[:, c], prior_ref.at[:, c], prior_sem.at[c]))
        copies.append(pltpu.make_async_copy(far_held.at[:, c], far_ref.at[:, c], far_sem.at[c]))
        copies[-2].start()
        copies[-1].start()
    for copy in copies:
        copy.wait()


def cross_tiles(place, own0, early, *late):
    in_hbm = pl.BlockSpec(memory_space=pltpu.HBM)
    prior_shape, far_shape = (2, 8, BLOCK, BLOCK), (2, 8, BLOCK, BLOCK // 2)
    lanes = late[0].shape[-1]
    return pl.pallas_call(
        cross_kernel,
        in_specs=[SMALL] + [IN_VMEM] * (2 + len(late)),
        out_specs=[in_hbm, in_hbm],
        out_shape=[pltpu.HBM(prior_shape, jnp.float32), pltpu.HBM(far_shape, jnp.float32)],
        scratch_shapes=[
            pltpu.VMEM((8, BLOCK, lanes), jnp.bfloat16),
            pltpu.VMEM((8, BLOCK + BLOCK // 2, lanes), jnp.bfloat16),
            pltpu.VMEM(prior_shape, jnp.float32),
            pltpu.VMEM(far_shape, jnp.float32),
            pltpu.SemaphoreType.DMA((8,)),
            pltpu.SemaphoreType.DMA((8,)),
        ],
        compiler_params=pltpu.CompilerParams(vmem_limit_bytes=20 * 1024 * 1024),
        name="cross_tiles",
    )(place, own0, early, *late)


CROSSED = [(0, 3), (1, 2), (2, 1), (3, 0)]
ODD_OVER = [(1, 2), (3, 0)]
EVEN_UP = [(0, 1), (2, 3)]
NEXT = [(0, 1), (1, 2), (2, 3), (3, 0)]
OVER = [(4, 7), (5, 6), (2, 1), (3, 0)]
ACROSS = [(4, 3), (5, 2), (2, 5), (3, 4)]
SWAPPED = [(0, 1), (1, 0), (2, 3), (3, 2)]


def on_device(table, order, samples, pfb_taps):
    position = lax.axis_index("narrow")
    place = jnp.stack([position // 2, position % 2, lax.axis_index("side")]).astype(jnp.int32)

    def exchange(crossing, rest, whole):
        f = lax.ppermute(crossing, "narrow", CROSSED)
        g = lax.ppermute(rest, "narrow", ODD_OVER)
        h = lax.ppermute(whole, "narrow", EVEN_UP)
        return f, g, h

    def swap(f):
        return lax.ppermute(f, "narrow", SWAPPED)

    (early,) = filter_section(place, samples, pfb_taps, table, 0, EARLY, False)
    stay, leave = filter_section(place, samples, pfb_taps, table, EARLY * SB, 1, True)
    source0 = lax.all_to_all(early, ("side", "plane"), split_axis=0, concat_axis=0, tiled=True)
    across = lax.ppermute(leave, ("side", "narrow"), ACROSS)
    over = lax.ppermute(stay, ("side", "narrow"), OVER)
    got = lax.ppermute(leave, "side", [(0, 1), (1, 0)])
    late = merge(place, stay, got, over, across)
    late, source0 = lax.optimization_barrier((late, source0))
    source1 = lax.all_to_all(late, "plane", split_axis=0, concat_axis=0, tiled=True)
    crossing0, rest0, own0 = early_rows(place, order, pltpu.with_memory_space_constraint(source0, pltpu.HBM))
    f0, g0, h0 = exchange(crossing0, rest0, own0)
    s0 = swap(f0)
    source1, f0 = lax.optimization_barrier((source1, f0))
    (rest1,) = late_rows(place, order, source1, True)
    r1 = lax.ppermute(rest1, "narrow", NEXT)
    source1, rest1 = lax.optimization_barrier((source1, rest1))
    crossing1, f1 = late_rows(place, order, source1, False)
    h1 = lax.ppermute(crossing1, "narrow", EVEN_UP)
    s1 = swap(f1)
    own0, crossing1, h1 = lax.optimization_barrier((own0, crossing1, h1))
    self_vis = self_tiles(place, own0, crossing1, rest1)
    held0 = early_columns(place, f0, g0, h0, s0)
    r1, self_vis, held0 = lax.optimization_barrier((r1, self_vis, held0))
    prior_vis, far_vis = cross_tiles(place, own0, held0, crossing1, rest1, f1, r1, h1, s1)
    return (self_vis, prior_vis, far_vis)


def solution(mesh):
    parted = Mesh(mesh.devices.reshape(2, mesh.devices.shape[0] // 2, mesh.devices.shape[1]), ("side", "plane", "narrow"))
    out_spec = P(None, ("side", "plane"), "narrow", None)
    return jax.shard_map(
        functools.partial(on_device, dft_table(), row_order()),
        mesh=parted,
        in_specs=(P(("narrow", "side", "plane"), None), P()),
        out_specs=(out_spec, out_spec, out_spec),
        check_vma=False,
    )
```

```python
import functools
import math

import jax
import jax.numpy as jnp
import numpy as np
from jax import lax
from jax.experimental import pallas as pl
from jax.experimental.pallas import tpu as pltpu
from jax.sharding import Mesh
from jax.sharding import PartitionSpec as P

CHAN = 512
TAPS = 4
SPECTRA = 384
BLOCK = 256
FRAME = 2 * CHAN
SB = 128
EARLY = 2
NT = (((1,), (1,)), ((), ()))
SMALL = pl.BlockSpec(memory_space=pltpu.SMEM)
IN_VMEM = pl.BlockSpec(memory_space=pltpu.VMEM)


def dft_table():
    positions = np.arange(FRAME, dtype=np.int32)
    bins = np.arange(CHAN, dtype=np.int32)
    phases = bins[:, None] * positions[None, :] % FRAME
    angles = phases.astype(np.float32) * np.float32(math.pi / CHAN)
    norming = np.float32(FRAME ** (-0.5))
    table = np.concatenate([np.cos(angles) * norming, -np.sin(angles) * norming])
    return table.astype(jnp.bfloat16)


def row_order():
    order = np.arange(256).reshape(32, 8).T.reshape(-1)
    return np.eye(256, dtype=np.float32)[order].astype(jnp.bfloat16)


def spectra_kernel(first, split, place_ref, x_ref, table_ref, taps_ref, *refs):
    outs, (x_held, table, taps_held, frames, filtered, out_held, x_sem, table_sem, taps_sem, out_sem) = refs[:-10], refs[-10:]
    blocks = x_held.shape[0]
    extra = TAPS - 1
    arriving = []
    for j in range(blocks):
        start, length = (first, SB + extra) if j == 0 else (first + j * SB + extra, SB)
        arriving.append(
            pltpu.make_async_copy(
                x_ref.at[:, pl.ds(start * FRAME, length * FRAME)], x_held.at[j, :, pl.ds(0, length * FRAME)], x_sem.at[j]
            )
        )
    table_arriving = pltpu.make_async_copy(table_ref, table, table_sem)
    taps_arriving = pltpu.make_async_copy(taps_ref, taps_held, taps_sem)
    taps_arriving.start()
    arriving[0].start()
    table_arriving.start()
    for copy in arriving[1:]:
        copy.start()
    taps_arriving.wait()
    leaving = []
    for j in range(blocks):
        arriving[j].wait()
        start, length = (0, SB + extra) if j == 0 else (j * SB + extra, SB)
        for f in range(length):
            for n in range(0, FRAME, 128):
                frames[n // 128, 4 * (start + f) : 4 * (start + f) + 4, :] = x_held[
                    j, :, f * FRAME + n : f * FRAME + n + 128
                ].astype(jnp.float32)
        for n in range(0, FRAME, 128):
            taps = [taps_held[t : t + 1, n : n + 128] for t in range(TAPS)]
            for i in range(4):
                for s in range(j * SB, (j + 1) * SB, 16):
                    total = frames[n // 128, pl.ds(i + 4 * s, 16, stride=4), :] * taps[0]
                    for t in range(1, TAPS):
                        total = total + frames[n // 128, pl.ds(i + 4 * (s + t), 16, stride=4), :] * taps[t]
                    row = i * SB + s - j * SB
                    filtered[row : row + 16, n : n + 128] = total.astype(jnp.bfloat16)
        if j == 0:
            table_arriving.wait()
        for pair in range(2):
            product = lax.dot_general(
                table[...], filtered[pair * 2 * SB : (pair + 1) * 2 * SB, :], NT, preferred_element_type=jnp.float32
            )
            for p in range(2):
                part = product[p * CHAN : (p + 1) * CHAN]
                rows = jnp.concatenate(
                    [part[:, :SB].reshape(CHAN // 8, 8, SB), part[:, SB:].reshape(CHAN // 8, 8, SB)], axis=1
                )
                out_held[j, :, pair * 16 : pair * 16 + 16, p * SB : (p + 1) * SB] = rows.astype(jnp.bfloat16)
        if split:
            side = place_ref[2]
            sources = [out_held.at[j, pl.ds(side * 32, 32)], out_held.at[j, pl.ds((1 - side) * 32, 32)]]
        else:
            sources = [out_held.at[j]]
        for k, (source, out) in enumerate(zip(sources, outs)):
            copy = pltpu.make_async_copy(source, out.at[:, :, pl.ds(j * 2 * SB, 2 * SB)], out_sem.at[2 * j + k])
            copy.start()
            leaving.append(copy)
    for copy in leaving:
        copy.wait()


def filter_section(place, samples, pfb_taps, table, first, blocks, split):
    in_hbm = pl.BlockSpec(memory_space=pltpu.HBM)
    lanes = blocks * 2 * SB
    out_shape = [pltpu.HBM((32, 32, lanes), jnp.bfloat16)] * 2 if split else [pltpu.HBM((64, 32, lanes), jnp.bfloat16)]
    return pl.pallas_call(
        functools.partial(spectra_kernel, first, split),
        in_specs=[SMALL, in_hbm, in_hbm, in_hbm],
        out_specs=[in_hbm] * len(out_shape),
        out_shape=out_shape,
        scratch_shapes=[
            pltpu.VMEM((blocks, 4, (SB + TAPS - 1) * FRAME), jnp.bfloat16),
            pltpu.VMEM((2 * CHAN, FRAME), jnp.bfloat16),
            pltpu.VMEM((TAPS, FRAME), jnp.float32),
            pltpu.VMEM((FRAME // 128, 4 * (blocks * SB + 4), 128), jnp.float32),
            pltpu.VMEM((4 * SB, FRAME), jnp.bfloat16),
            pltpu.VMEM((blocks, 64, 32, 2 * SB), jnp.bfloat16),
            pltpu.SemaphoreType.DMA((blocks,)),
            pltpu.SemaphoreType.DMA,
            pltpu.SemaphoreType.DMA,
            pltpu.SemaphoreType.DMA((2 * blocks,)),
        ],
        compiler_params=pltpu.CompilerParams(vmem_limit_bytes=20 * 1024 * 1024),
        name="filter_section",
    )(place, *(pltpu.with_memory_space_constraint(a, pltpu.HBM) for a in (samples, table, pfb_taps)))


def merge_kernel(place_ref, stay_ref, got_ref, out_ref, held, sem):
    side = place_ref[2]
    held[:, side] = stay_ref[...]
    held[:, 1 - side] = got_ref[...]
    copy = pltpu.make_async_copy(held, out_ref, sem)
    copy.start()
    copy.wait()


def merge(place, stay, got):
    shape = (32, 2) + stay.shape[1:]
    return pl.pallas_call(
        merge_kernel,
        in_specs=[SMALL, IN_VMEM, IN_VMEM],
        out_specs=pl.BlockSpec(memory_space=pltpu.HBM),
        out_shape=pltpu.HBM(shape, jnp.bfloat16),
        scratch_shapes=[pltpu.VMEM(shape, jnp.bfloat16), pltpu.SemaphoreType.DMA],
        compiler_params=pltpu.CompilerParams(vmem_limit_bytes=8 * 1024 * 1024),
        name="merge_sides",
    )(place, stay, got)


def rows_kernel(crossing, place_ref, order_ref, source_ref, out_ref, source, held, in_sem, out_sem):
    half = 1 - place_ref[0] if crossing else place_ref[0]
    part = source_ref.at[pl.ds(half * 32, 32)] if len(source_ref.shape) == 3 else source_ref.at[:, half]
    arriving = pltpu.make_async_copy(part, source, in_sem)
    arriving.start()
    arriving.wait()
    for g in range(4):
        rows = source[g * 8 : (g + 1) * 8].reshape(256, source.shape[-1])
        turned = jnp.dot(order_ref[...], rows, preferred_element_type=jnp.float32).astype(jnp.bfloat16)
        for c in range(8):
            held[c, g * 32 : (g + 1) * 32, :] = turned[c * 32 : (c + 1) * 32]
    leaving = pltpu.make_async_copy(held, out_ref, out_sem)
    leaving.start()
    leaving.wait()


def channel_rows(place, order, source, crossing):
    lanes = source.shape[-1]
    return pl.pallas_call(
        functools.partial(rows_kernel, crossing),
        in_specs=[SMALL, IN_VMEM, pl.BlockSpec(memory_space=pl.ANY)],
        out_specs=pl.BlockSpec(memory_space=pltpu.HBM),
        out_shape=pltpu.HBM((8, 128, lanes), jnp.bfloat16),
        scratch_shapes=[
            pltpu.VMEM((32, 32, lanes), jnp.bfloat16),
            pltpu.VMEM((8, 128, lanes), jnp.bfloat16),
            pltpu.SemaphoreType.DMA,
            pltpu.SemaphoreType.DMA,
        ],
        compiler_params=pltpu.CompilerParams(vmem_limit_bytes=12 * 1024 * 1024),
        name="channel_rows",
    )(place, order, source)


def stacked(rows):
    pieces = []
    for s in range(0, rows.shape[1], 2 * SB):
        pieces += [rows[:, s + SB : s + 2 * SB], -rows[:, s : s + SB]]
    return jnp.concatenate([rows, jnp.concatenate(pieces, axis=1)], axis=0)


def tile_products(rows, cols):
    return lax.dot_general(stacked(rows), cols, NT, preferred_element_type=jnp.float32)


def put_halves(place_ref, chips_ref, others_ref, out_ref, lane=0):
    chip = place_ref[0]
    lanes = slice(lane, lane + chips_ref.shape[-1])
    out_ref[:, pl.ds(pl.multiple_of(chip * 128, 128), 128), lanes] = chips_ref[...]
    out_ref[:, pl.ds(pl.multiple_of((1 - chip) * 128, 128), 128), lanes] = others_ref[...]


def self_kernel(place_ref, crossing0_ref, rest0_ref, crossing1_ref, rest1_ref, self_ref, own, self_held, sem):
    put_halves(place_ref, rest0_ref, crossing0_ref, own)
    put_halves(place_ref, rest1_ref, crossing1_ref, own, rest0_ref.shape[-1])
    copies = []
    for c in range(8):
        product = tile_products(own[c], own[c]) * (1.0 / SPECTRA)
        self_held[0, c] = product[:BLOCK]
        self_held[1, c] = product[BLOCK:]
        copies.append(pltpu.make_async_copy(self_held.at[:, c], self_ref.at[:, c], sem.at[c]))
        copies[-1].start()
    for copy in copies:
        copy.wait()


def self_tiles(place, *own):
    return pl.pallas_call(
        self_kernel,
        in_specs=[SMALL] + [IN_VMEM] * 4,
        out_specs=pl.BlockSpec(memory_space=pltpu.HBM),
        out_shape=pltpu.HBM((2, 8, BLOCK, BLOCK), jnp.float32),
        scratch_shapes=[
            pltpu.VMEM((8, BLOCK, own[0].shape[-1] + own[2].shape[-1]), jnp.bfloat16),
            pltpu.VMEM((2, 8, BLOCK, BLOCK), jnp.float32),
            pltpu.SemaphoreType.DMA((8,)),
        ],
        compiler_params=pltpu.CompilerParams(vmem_limit_bytes=14 * 1024 * 1024),
        name="self_tiles",
    )(place, *own)


def put_columns(place_ref, f_ref, r_ref, h_ref, s_ref, out_ref):
    @pl.when(place_ref[1] == 0)
    def _():
        put_halves(place_ref, f_ref, r_ref, out_ref)

    @pl.when(place_ref[1] == 1)
    def _():
        put_halves(place_ref, r_ref, h_ref, out_ref)

    out_ref[:, BLOCK:, :] = s_ref[...]


def early_kernel(place_ref, crossing_ref, rest_ref, f_ref, r_ref, h_ref, s_ref, out_ref, own, held):
    put_halves(place_ref, rest_ref, crossing_ref, own)
    put_columns(place_ref, f_ref, r_ref, h_ref, s_ref, held)
    for c in range(8):
        out_ref[c] = tile_products(own[c], held[c])


def early_products(place, *chunk):
    columns, lanes = BLOCK + BLOCK // 2, chunk[0].shape[-1]
    return pl.pallas_call(
        early_kernel,
        in_specs=[SMALL] + [IN_VMEM] * 6,
        out_specs=IN_VMEM,
        out_shape=jax.ShapeDtypeStruct((8, 2 * BLOCK, columns), jnp.float32),
        scratch_shapes=[pltpu.VMEM((8, BLOCK, lanes), jnp.bfloat16), pltpu.VMEM((8, columns, lanes), jnp.bfloat16)],
        compiler_params=pltpu.CompilerParams(vmem_limit_bytes=14 * 1024 * 1024),
        name="early_products",
    )(place, *chunk)


def cross_kernel(place_ref, early_ref, crossing_ref, rest_ref, f_ref, r_ref, h_ref, s_ref, prior_ref, far_ref,
                 own, held, prior_held, far_held, prior_sem, far_sem):
    put_halves(place_ref, rest_ref, crossing_ref, own)
    put_columns(place_ref, f_ref, r_ref, h_ref, s_ref, held)
    copies = []
    for c in range(8):
        product = (tile_products(own[c], held[c]) + early_ref[c]) * (1.0 / SPECTRA)
        for p in range(2):
            prior_held[p, c] = product[p * BLOCK : (p + 1) * BLOCK, :BLOCK]
            far_held[p, c] = product[p * BLOCK : (p + 1) * BLOCK, BLOCK:]
        copies.append(pltpu.make_async_copy(prior_held.at[:, c], prior_ref.at[:, c], prior_sem.at[c]))
        copies.append(pltpu.make_async_copy(far_held.at[:, c], far_ref.at[:, c], far_sem.at[c]))
        copies[-2].start()
        copies[-1].start()
    for copy in copies:
        copy.wait()


def cross_tiles(place, early, *chunk):
    in_hbm = pl.BlockSpec(memory_space=pltpu.HBM)
    prior_shape, far_shape = (2, 8, BLOCK, BLOCK), (2, 8, BLOCK, BLOCK // 2)
    lanes = chunk[0].shape[-1]
    return pl.pallas_call(
        cross_kernel,
        in_specs=[SMALL] + [IN_VMEM] * 7,
        out_specs=[in_hbm, in_hbm],
        out_shape=[pltpu.HBM(prior_shape, jnp.float32), pltpu.HBM(far_shape, jnp.float32)],
        scratch_shapes=[
            pltpu.VMEM((8, BLOCK, lanes), jnp.bfloat16),
            pltpu.VMEM((8, BLOCK + BLOCK // 2, lanes), jnp.bfloat16),
            pltpu.VMEM(prior_shape, jnp.float32),
            pltpu.VMEM(far_shape, jnp.float32),
            pltpu.SemaphoreType.DMA((8,)),
            pltpu.SemaphoreType.DMA((8,)),
        ],
        compiler_params=pltpu.CompilerParams(vmem_limit_bytes=20 * 1024 * 1024),
        name="cross_tiles",
    )(place, early, *chunk)


CROSSED = [(0, 3), (1, 2), (2, 1), (3, 0)]
NEXT = [(0, 1), (1, 2), (2, 3), (3, 0)]
EVEN_UP = [(0, 1), (2, 3)]
SWAPPED = [(0, 1), (1, 0), (2, 3), (3, 2)]


def on_device(table, order, samples, pfb_taps):
    position = lax.axis_index("narrow")
    place = jnp.stack([position // 2, position % 2, lax.axis_index("side")]).astype(jnp.int32)

    def swap(f):
        return lax.ppermute(f, "narrow", SWAPPED)

    (early,) = filter_section(place, samples, pfb_taps, table, 0, EARLY, False)
    stay, leave = filter_section(place, samples, pfb_taps, table, EARLY * SB, 1, True)
    source0 = lax.all_to_all(early, ("side", "plane"), split_axis=0, concat_axis=0, tiled=True)
    late = merge(place, stay, lax.ppermute(leave, "side", [(0, 1), (1, 0)]))
    late, source0 = lax.optimization_barrier((late, source0))
    source1 = lax.all_to_all(late, "plane", split_axis=0, concat_axis=0, tiled=True)
    crossing0 = channel_rows(place, order, source0, True)
    f0 = lax.ppermute(crossing0, "narrow", CROSSED)
    rest0 = channel_rows(place, order, source0, False)
    r0 = lax.ppermute(rest0, "narrow", NEXT)
    h0 = lax.ppermute(crossing0, "narrow", EVEN_UP)
    f0, rest0 = lax.optimization_barrier((f0, rest0))
    s0 = swap(f0)
    source1, f0, h0, s0 = lax.optimization_barrier((source1, f0, h0, s0))
    crossing1 = channel_rows(place, order, source1, True)
    f1 = lax.ppermute(crossing1, "narrow", CROSSED)
    rest1 = channel_rows(place, order, source1, False)
    r1 = lax.ppermute(rest1, "narrow", NEXT)
    h1 = lax.ppermute(crossing1, "narrow", EVEN_UP)
    crossing1, r0, h1 = lax.optimization_barrier((crossing1, r0, h1))
    early = early_products(place, crossing0, rest0, f0, r0, h0, s0)
    self_vis = self_tiles(place, crossing0, rest0, crossing1, rest1)
    f1, self_vis, early = lax.optimization_barrier((f1, self_vis, early))
    prior_vis, far_vis = cross_tiles(place, early, crossing1, rest1, f1, r1, h1, swap(f1))
    return (self_vis, prior_vis, far_vis)


def solution(mesh):
    parted = Mesh(mesh.devices.reshape(2, mesh.devices.shape[0] // 2, mesh.devices.shape[1]), ("side", "plane", "narrow"))
    out_spec = P(None, ("side", "plane"), "narrow", None)
    return jax.shard_map(
        functools.partial(on_device, dft_table(), row_order()),
        mesh=parted,
        in_specs=(P(("narrow", "side", "plane"), None), P()),
        out_specs=(out_spec, out_spec, out_spec),
        check_vma=False,
    )
```

```python
import functools
import math

import jax
import jax.numpy as jnp
import numpy as np
from jax import lax
from jax.experimental import pallas as pl
from jax.experimental.pallas import tpu as pltpu
from jax.sharding import Mesh
from jax.sharding import PartitionSpec as P

CHAN = 512
TAPS = 4
SPECTRA = 384
BLOCK = 256
FRAME = 2 * CHAN
SB = 128
EARLY = 2
NT = (((1,), (1,)), ((), ()))
SMALL = pl.BlockSpec(memory_space=pltpu.SMEM)
IN_VMEM = pl.BlockSpec(memory_space=pltpu.VMEM)


def dft_table():
    positions = np.arange(FRAME, dtype=np.int32)
    bins = np.arange(CHAN, dtype=np.int32)
    phases = bins[:, None] * positions[None, :] % FRAME
    angles = phases.astype(np.float32) * np.float32(math.pi / CHAN)
    norming = np.float32(FRAME ** (-0.5))
    table = np.concatenate([np.cos(angles) * norming, -np.sin(angles) * norming])
    return table.astype(jnp.bfloat16)


def row_order():
    order = np.arange(256).reshape(32, 8).T.reshape(-1)
    return np.eye(256, dtype=np.float32)[order].astype(jnp.bfloat16)


def spectra_kernel(first, split, place_ref, x_ref, table_ref, taps_ref, *refs):
    outs, (x_held, table, taps_held, frames, filtered, out_held, x_sem, table_sem, taps_sem, out_sem) = refs[:-10], refs[-10:]
    blocks = x_held.shape[0]
    extra = TAPS - 1
    arriving = []
    for j in range(blocks):
        start, length = (first, SB + extra) if j == 0 else (first + j * SB + extra, SB)
        arriving.append(
            pltpu.make_async_copy(
                x_ref.at[:, pl.ds(start * FRAME, length * FRAME)], x_held.at[j, :, pl.ds(0, length * FRAME)], x_sem.at[j]
            )
        )
    table_arriving = pltpu.make_async_copy(table_ref, table, table_sem)
    taps_arriving = pltpu.make_async_copy(taps_ref, taps_held, taps_sem)
    taps_arriving.start()
    arriving[0].start()
    table_arriving.start()
    for copy in arriving[1:]:
        copy.start()
    taps_arriving.wait()
    leaving = []
    for j in range(blocks):
        arriving[j].wait()
        start, length = (0, SB + extra) if j == 0 else (j * SB + extra, SB)
        for f in range(length):
            for n in range(0, FRAME, 128):
                frames[n // 128, 4 * (start + f) : 4 * (start + f) + 4, :] = x_held[
                    j, :, f * FRAME + n : f * FRAME + n + 128
                ].astype(jnp.float32)
        for n in range(0, FRAME, 128):
            taps = [taps_held[t : t + 1, n : n + 128] for t in range(TAPS)]
            for i in range(4):
                for s in range(j * SB, (j + 1) * SB, 16):
                    total = frames[n // 128, pl.ds(i + 4 * s, 16, stride=4), :] * taps[0]
                    for t in range(1, TAPS):
                        total = total + frames[n // 128, pl.ds(i + 4 * (s + t), 16, stride=4), :] * taps[t]
                    row = i * SB + s - j * SB
                    filtered[row : row + 16, n : n + 128] = total.astype(jnp.bfloat16)
        if j == 0:
            table_arriving.wait()
        for pair in range(2):
            product = lax.dot_general(
                table[...], filtered[pair * 2 * SB : (pair + 1) * 2 * SB, :], NT, preferred_element_type=jnp.float32
            )
            for p in range(2):
                part = product[p * CHAN : (p + 1) * CHAN]
                rows = jnp.concatenate(
                    [part[:, :SB].reshape(CHAN // 8, 8, SB), part[:, SB:].reshape(CHAN // 8, 8, SB)], axis=1
                )
                out_held[j, :, pair * 16 : pair * 16 + 16, p * SB : (p + 1) * SB] = rows.astype(jnp.bfloat16)
        if split:
            side = place_ref[2]
            sources = [out_held.at[j, pl.ds(side * 32, 32)], out_held.at[j, pl.ds((1 - side) * 32, 32)]]
        else:
            sources = [out_held.at[j]]
        for k, (source, out) in enumerate(zip(sources, outs)):
            copy = pltpu.make_async_copy(source, out.at[:, :, pl.ds(j * 2 * SB, 2 * SB)], out_sem.at[2 * j + k])
            copy.start()
            leaving.append(copy)
    for copy in leaving:
        copy.wait()


def filter_section(place, samples, pfb_taps, table, first, blocks, split):
    in_hbm = pl.BlockSpec(memory_space=pltpu.HBM)
    lanes = blocks * 2 * SB
    out_shape = [pltpu.HBM((32, 32, lanes), jnp.bfloat16)] * 2 if split else [pltpu.HBM((64, 32, lanes), jnp.bfloat16)]
    return pl.pallas_call(
        functools.partial(spectra_kernel, first, split),
        in_specs=[SMALL, in_hbm, in_hbm, in_hbm],
        out_specs=[in_hbm] * len(out_shape),
        out_shape=out_shape,
        scratch_shapes=[
            pltpu.VMEM((blocks, 4, (SB + TAPS - 1) * FRAME), jnp.bfloat16),
            pltpu.VMEM((2 * CHAN, FRAME), jnp.bfloat16),
            pltpu.VMEM((TAPS, FRAME), jnp.float32),
            pltpu.VMEM((FRAME // 128, 4 * (blocks * SB + 4), 128), jnp.float32),
            pltpu.VMEM((4 * SB, FRAME), jnp.bfloat16),
            pltpu.VMEM((blocks, 64, 32, 2 * SB), jnp.bfloat16),
            pltpu.SemaphoreType.DMA((blocks,)),
            pltpu.SemaphoreType.DMA,
            pltpu.SemaphoreType.DMA,
            pltpu.SemaphoreType.DMA((2 * blocks,)),
        ],
        compiler_params=pltpu.CompilerParams(vmem_limit_bytes=20 * 1024 * 1024),
        name="filter_section",
    )(place, *(pltpu.with_memory_space_constraint(a, pltpu.HBM) for a in (samples, table, pfb_taps)))


def merge_kernel(place_ref, stay_ref, got_ref, out_ref, held, sem):
    side = place_ref[2]
    held[:, side] = stay_ref[...]
    held[:, 1 - side] = got_ref[...]
    copy = pltpu.make_async_copy(held, out_ref, sem)
    copy.start()
    copy.wait()


def merge(place, stay, got):
    shape = (32, 2) + stay.shape[1:]
    return pl.pallas_call(
        merge_kernel,
        in_specs=[SMALL, IN_VMEM, IN_VMEM],
        out_specs=pl.BlockSpec(memory_space=pltpu.HBM),
        out_shape=pltpu.HBM(shape, jnp.bfloat16),
        scratch_shapes=[pltpu.VMEM(shape, jnp.bfloat16), pltpu.SemaphoreType.DMA],
        compiler_params=pltpu.CompilerParams(vmem_limit_bytes=8 * 1024 * 1024),
        name="merge_sides",
    )(place, stay, got)


def rows_kernel(crossing, place_ref, order_ref, source_ref, out_ref, source, held, in_sem, out_sem):
    half = 1 - place_ref[0] if crossing else place_ref[0]
    part = source_ref.at[pl.ds(half * 32, 32)] if len(source_ref.shape) == 3 else source_ref.at[:, half]
    arriving = pltpu.make_async_copy(part, source, in_sem)
    arriving.start()
    arriving.wait()
    for g in range(4):
        rows = source[g * 8 : (g + 1) * 8].reshape(256, source.shape[-1])
        turned = jnp.dot(order_ref[...], rows, preferred_element_type=jnp.float32).astype(jnp.bfloat16)
        for c in range(8):
            held[c, g * 32 : (g + 1) * 32, :] = turned[c * 32 : (c + 1) * 32]
    leaving = pltpu.make_async_copy(held, out_ref, out_sem)
    leaving.start()
    leaving.wait()


def channel_rows(place, order, source, crossing):
    lanes = source.shape[-1]
    return pl.pallas_call(
        functools.partial(rows_kernel, crossing),
        in_specs=[SMALL, IN_VMEM, pl.BlockSpec(memory_space=pl.ANY)],
        out_specs=pl.BlockSpec(memory_space=pltpu.HBM),
        out_shape=pltpu.HBM((8, 128, lanes), jnp.bfloat16),
        scratch_shapes=[
            pltpu.VMEM((32, 32, lanes), jnp.bfloat16),
            pltpu.VMEM((8, 128, lanes), jnp.bfloat16),
            pltpu.SemaphoreType.DMA,
            pltpu.SemaphoreType.DMA,
        ],
        compiler_params=pltpu.CompilerParams(vmem_limit_bytes=12 * 1024 * 1024),
        name="channel_rows",
    )(place, order, source)


def stacked(rows):
    pieces = []
    for s in range(0, rows.shape[1], 2 * SB):
        pieces += [rows[:, s + SB : s + 2 * SB], -rows[:, s : s + SB]]
    return jnp.concatenate([rows, jnp.concatenate(pieces, axis=1)], axis=0)


def tile_products(rows, cols):
    return lax.dot_general(stacked(rows), cols, NT, preferred_element_type=jnp.float32)


def put_halves(place_ref, chips_ref, others_ref, out_ref, lane=0):
    chip = place_ref[0]
    lanes = slice(lane, lane + chips_ref.shape[-1])
    out_ref[:, pl.ds(pl.multiple_of(chip * 128, 128), 128), lanes] = chips_ref[...]
    out_ref[:, pl.ds(pl.multiple_of((1 - chip) * 128, 128), 128), lanes] = others_ref[...]


def self_kernel(place_ref, crossing0_ref, rest0_ref, crossing1_ref, rest1_ref, self_ref, own, self_held, sem):
    put_halves(place_ref, rest0_ref, crossing0_ref, own)
    put_halves(place_ref, rest1_ref, crossing1_ref, own, rest0_ref.shape[-1])
    copies = []
    for c in range(8):
        product = tile_products(own[c], own[c]) * (1.0 / SPECTRA)
        self_held[0, c] = product[:BLOCK]
        self_held[1, c] = product[BLOCK:]
        copies.append(pltpu.make_async_copy(self_held.at[:, c], self_ref.at[:, c], sem.at[c]))
        copies[-1].start()
    for copy in copies:
        copy.wait()


def self_tiles(place, *own):
    return pl.pallas_call(
        self_kernel,
        in_specs=[SMALL] + [IN_VMEM] * 4,
        out_specs=pl.BlockSpec(memory_space=pltpu.HBM),
        out_shape=pltpu.HBM((2, 8, BLOCK, BLOCK), jnp.float32),
        scratch_shapes=[
            pltpu.VMEM((8, BLOCK, own[0].shape[-1] + own[2].shape[-1]), jnp.bfloat16),
            pltpu.VMEM((2, 8, BLOCK, BLOCK), jnp.float32),
            pltpu.SemaphoreType.DMA((8,)),
        ],
        compiler_params=pltpu.CompilerParams(vmem_limit_bytes=14 * 1024 * 1024),
        name="self_tiles",
    )(place, *own)


def put_columns(place_ref, f_ref, r_ref, h_ref, s_ref, out_ref):
    @pl.when(place_ref[1] == 0)
    def _():
        put_halves(place_ref, f_ref, r_ref, out_ref)

    @pl.when(place_ref[1] == 1)
    def _():
        put_halves(place_ref, r_ref, h_ref, out_ref)

    out_ref[:, BLOCK:, :] = s_ref[...]


def early_kernel(place_ref, crossing_ref, rest_ref, f_ref, r_ref, h_ref, s_ref, out_ref, own, held):
    put_halves(place_ref, rest_ref, crossing_ref, own)
    put_columns(place_ref, f_ref, r_ref, h_ref, s_ref, held)
    for c in range(8):
        out_ref[c] = tile_products(own[c], held[c])


def early_products(place, *chunk):
    columns, lanes = BLOCK + BLOCK // 2, chunk[0].shape[-1]
    return pl.pallas_call(
        early_kernel,
        in_specs=[SMALL] + [IN_VMEM] * 6,
        out_specs=IN_VMEM,
        out_shape=jax.ShapeDtypeStruct((8, 2 * BLOCK, columns), jnp.float32),
        scratch_shapes=[pltpu.VMEM((8, BLOCK, lanes), jnp.bfloat16), pltpu.VMEM((8, columns, lanes), jnp.bfloat16)],
        compiler_params=pltpu.CompilerParams(vmem_limit_bytes=14 * 1024 * 1024),
        name="early_products",
    )(place, *chunk)


def cross_kernel(place_ref, early_ref, crossing_ref, rest_ref, f_ref, r_ref, h_ref, s_ref, prior_ref, far_ref,
                 own, held, prior_held, far_held, prior_sem, far_sem):
    put_halves(place_ref, rest_ref, crossing_ref, own)
    put_columns(place_ref, f_ref, r_ref, h_ref, s_ref, held)
    copies = []
    for c in range(8):
        product = (tile_products(own[c], held[c]) + early_ref[c]) * (1.0 / SPECTRA)
        for p in range(2):
            prior_held[p, c] = product[p * BLOCK : (p + 1) * BLOCK, :BLOCK]
            far_held[p, c] = product[p * BLOCK : (p + 1) * BLOCK, BLOCK:]
        copies.append(pltpu.make_async_copy(prior_held.at[:, c], prior_ref.at[:, c], prior_sem.at[c]))
        copies.append(pltpu.make_async_copy(far_held.at[:, c], far_ref.at[:, c], far_sem.at[c]))
        copies[-2].start()
        copies[-1].start()
    for copy in copies:
        copy.wait()


def cross_tiles(place, early, *chunk):
    in_hbm = pl.BlockSpec(memory_space=pltpu.HBM)
    prior_shape, far_shape = (2, 8, BLOCK, BLOCK), (2, 8, BLOCK, BLOCK // 2)
    lanes = chunk[0].shape[-1]
    return pl.pallas_call(
        cross_kernel,
        in_specs=[SMALL] + [IN_VMEM] * 7,
        out_specs=[in_hbm, in_hbm],
        out_shape=[pltpu.HBM(prior_shape, jnp.float32), pltpu.HBM(far_shape, jnp.float32)],
        scratch_shapes=[
            pltpu.VMEM((8, BLOCK, lanes), jnp.bfloat16),
            pltpu.VMEM((8, BLOCK + BLOCK // 2, lanes), jnp.bfloat16),
            pltpu.VMEM(prior_shape, jnp.float32),
            pltpu.VMEM(far_shape, jnp.float32),
            pltpu.SemaphoreType.DMA((8,)),
            pltpu.SemaphoreType.DMA((8,)),
        ],
        compiler_params=pltpu.CompilerParams(vmem_limit_bytes=20 * 1024 * 1024),
        name="cross_tiles",
    )(place, early, *chunk)


CROSSED = [(0, 3), (1, 2), (2, 1), (3, 0)]
NEXT = [(0, 1), (1, 2), (2, 3), (3, 0)]
EVEN_UP = [(0, 1), (2, 3)]
SWAPPED = [(0, 1), (1, 0), (2, 3), (3, 2)]


def on_device(table, order, samples, pfb_taps):
    position = lax.axis_index("narrow")
    place = jnp.stack([position // 2, position % 2, lax.axis_index("side")]).astype(jnp.int32)

    def swap(f):
        return lax.ppermute(f, "narrow", SWAPPED)

    (early,) = filter_section(place, samples, pfb_taps, table, 0, EARLY, False)
    stay, leave = filter_section(place, samples, pfb_taps, table, EARLY * SB, 1, True)
    source0 = lax.all_to_all(early, ("side", "plane"), split_axis=0, concat_axis=0, tiled=True)
    late = merge(place, stay, lax.ppermute(leave, "side", [(0, 1), (1, 0)]))
    late, source0 = lax.optimization_barrier((late, source0))
    source1 = lax.all_to_all(late, "plane", split_axis=0, concat_axis=0, tiled=True)
    crossing0 = channel_rows(place, order, source0, True)
    f0 = lax.ppermute(crossing0, "narrow", CROSSED)
    rest0 = channel_rows(place, order, source0, False)
    r0 = lax.ppermute(rest0, "narrow", NEXT)
    h0 = lax.ppermute(crossing0, "narrow", EVEN_UP)
    f0, rest0 = lax.optimization_barrier((f0, rest0))
    s0 = swap(f0)
    source1, f0, h0, s0 = lax.optimization_barrier((source1, f0, h0, s0))
    crossing1 = channel_rows(place, order, source1, True)
    f1 = lax.ppermute(crossing1, "narrow", CROSSED)
    rest1 = channel_rows(place, order, source1, False)
    r1 = lax.ppermute(rest1, "narrow", NEXT)
    h1 = lax.ppermute(crossing1, "narrow", EVEN_UP)
    crossing1, r0 = lax.optimization_barrier((crossing1, r0))
    early = early_products(place, crossing0, rest0, f0, r0, h0, s0)
    self_vis = self_tiles(place, crossing0, rest0, crossing1, rest1)
    f1, self_vis, early = lax.optimization_barrier((f1, self_vis, early))
    prior_vis, far_vis = cross_tiles(place, early, crossing1, rest1, f1, r1, h1, swap(f1))
    return (self_vis, prior_vis, far_vis)


def solution(mesh):
    parted = Mesh(mesh.devices.reshape(2, mesh.devices.shape[0] // 2, mesh.devices.shape[1]), ("side", "plane", "narrow"))
    out_spec = P(None, ("side", "plane"), "narrow", None)
    return jax.shard_map(
        functools.partial(on_device, dft_table(), row_order()),
        mesh=parted,
        in_specs=(P(("narrow", "side", "plane"), None), P()),
        out_specs=(out_spec, out_spec, out_spec),
        check_vma=False,
    )
```
